128 devices in a mesh: grp: 8 (over y, core), dev: 16 (over z, x).
Axes of the slice: x: 4, y: 4, z: 4, core: 2. Of those that a mesh axis runs over, the one named last changes fastest.
Arguments:
- slab: bfloat16 [262144, 4096], P(('grp', 'dev')), may hold values from -1000 to 1000
- sketch_map: bfloat16 [4096, 320], replicated, may hold values from -0.09375 to 0.09375
Outputs:
- basis: float32 [262144, 320], P(('grp', 'dev'))
- coeffs: float32 [320, 4096], P(None, 'dev')
The draws below stay inside these ranges and needn't reach their ends.
All inputs are finite; a program needn't handle non-finite values.
Results may differ from the reference program's by a relative error of at most 0.0022.
Values sent between devices are 32-bit elements; how exact they have to be, the bound alone decides.
A program may use at most 128 MiB of HBM per device.

```python
import math
import jax
import jax.numpy as jnp
from jax import lax

N = 4096
SKETCH = 320
ROWS = 262144
N_GRP = 8
N_DEV = 16


def draw_slab(key, part):
    key = jax.random.fold_in(key, 11)
    keys = jax.random.split(key, 3)
    place = jnp.arange(ROWS, dtype=jnp.float32).reshape(ROWS, 1) / (ROWS - 1)
    row_level = jax.random.uniform(keys[0], (ROWS, 1), jnp.float32)
    col_level = jax.random.uniform(keys[1], (1, N), jnp.float32)
    col_scale = jnp.power(10.0, col_level - 0.5)
    row_scale = (1.0 + 2.0 * place) * jnp.power(10.0, row_level) / 4.0
    entries = jnp.clip(jax.random.normal(keys[2], (ROWS, N), jnp.float32), -6.0, 6.0)
    values = jnp.clip(entries * row_scale * col_scale, -1000.0, 1000.0)
    return values.astype(jnp.bfloat16)


def scatter_about(own_key, extent, scale, most, held_as=jnp.bfloat16):
    values = scale * jax.random.normal(own_key, extent, jnp.float32)
    return jnp.clip(values, min=-most, max=most).astype(held_as)


def setup_inputs(seed: int = 0) -> dict:
    key_list = jax.random.split(jax.random.key(seed), 3)
    return {
        "slab": draw_slab(jax.random.fold_in(key_list[2], 71), 0),
        "sketch_map": scatter_about(key_list[1], (N, SKETCH), N ** -0.5, 0.09375),
    }


def reference(slab, sketch_map):
    rows = slab.shape[0]
    scale = math.sqrt(rows)
    sketch = jnp.dot(slab.astype(jnp.float32), sketch_map.astype(jnp.float32), preferred_element_type=jnp.float32)
    gram = jnp.dot(sketch.T, sketch, precision=lax.Precision.HIGHEST)
    lower = jnp.linalg.cholesky(gram)
    basis = lax.linalg.triangular_solve(lower, sketch.T, left_side=True, lower=True).T * scale
    blocks = N_GRP * N_DEV

    def add_block(total, pair):
        sketch_block, slab_block = pair
        term = jnp.dot(sketch_block.T, slab_block.astype(jnp.float32), precision=lax.Precision.HIGHEST)
        return (total + term, None)
    cross, unused = lax.scan(add_block, jnp.zeros((SKETCH, N), jnp.float32), (sketch.reshape(blocks, -1, SKETCH), slab.reshape(blocks, -1, N)))
    coeffs = lax.linalg.triangular_solve(lower, cross, left_side=True, lower=True) / scale
    return (basis, coeffs)
```

```python
import math

import jax
import jax.numpy as jnp
from jax import lax
from jax.experimental import pallas as pl
from jax.experimental.pallas import tpu as pltpu
from jax.sharding import PartitionSpec as P

F32 = jnp.float32
BF16 = jnp.bfloat16
NN = (((1,), (0,)), ((), ()))
NT = (((1,), (1,)), ((), ()))
TN = (((0,), (0,)), ((), ()))
MESH = pl.DeviceIdType.MESH

N = 4096
SK = 320
HALF = SK // 2
LOCAL = 2048
CHUNK = 512
WIDTH = 256
SLICES = 16
SIDE = 4
TILES = 96
PIECE = TILES // 32


def dot(a, b, dims):
    return lax.dot_general(a, b, dims, preferred_element_type=F32)


def split(a):
    high = a.astype(BF16)
    return high, (a - high.astype(F32)).astype(BF16)


def dot3(a, b, dims):
    ah, al = split(a)
    bh, bl = split(b)
    return dot(ah, bh, dims) + (dot(ah, bl, dims) + dot(al, bh, dims))


def factor_block(a, n, w):
    eye = lax.broadcasted_iota(jnp.int32, (n, n), 0) == lax.broadcasted_iota(jnp.int32, (n, n), 1)
    m = jnp.concatenate([a, eye.astype(F32)], axis=1)
    width = 2 * n
    row_in_group = lax.broadcasted_iota(jnp.int32, (8, width), 0)
    per = w // 8
    groups = [m[8 * g : 8 * g + 8] for g in range(n // 8)]
    done = []
    for p in range(n // w):
        rows = groups[p * per : (p + 1) * per]
        cols = [
            [jnp.broadcast_to(r[:, p * w + l : p * w + l + 1], (8, width)) for r in rows]
            for l in range(w)
        ]
        pivots = [jnp.ones((8, width), F32) for _ in rows]
        for k in range(w):
            g, i = divmod(k, 8)
            pivot = jnp.broadcast_to(cols[k][g][i : i + 1], (8, width))
            inverse = 1.0 / pivot
            factor = {}
            for h in range(g, per):
                factor[h] = cols[k][h] * inverse
            factor[g] = jnp.where(row_in_group > i, factor[g], 0.0)
            for l in range(k + 1, w):
                value = jnp.broadcast_to(cols[l][g][i : i + 1], (8, width))
                for h in range(g, per):
                    cols[l][h] = cols[l][h] - factor[h] * value
            value = jnp.broadcast_to(rows[g][i : i + 1], (8, width))
            for h in range(g, per):
                rows[h] = rows[h] - factor[h] * value
            pivots[g] = jnp.where(row_in_group == i, pivot, pivots[g])
        block = jnp.concatenate([r * lax.rsqrt(v) for r, v in zip(rows, pivots)], axis=0)
        done.append(block[:, n:])
        if p < n // w - 1:
            high, low = split(block)
            left = jnp.concatenate([high, low, high], axis=0)[:, :n]
            right = jnp.concatenate([high, high, low], axis=0)
            update = dot(left, right, TN)
            for g in range((p + 1) * per, n // 8):
                groups[g] = groups[g] - update[8 * g : 8 * g + 8]
    return jnp.concatenate(done, axis=0)


def invert_factor(m, n, b, w):
    for k in range(n // b):
        lo, hi = k * b, (k + 1) * b
        t = factor_block(m[lo:hi, lo:hi], b, w)
        r = dot3(t, m[lo:hi, :], NN)
        parts = [r[:, :lo]] if lo else []
        parts.append(t)
        if hi < n:
            parts.append(r[:, hi:])
        r = jnp.concatenate(parts, axis=1)
        if hi < n:
            col = lax.broadcasted_iota(jnp.int32, (n - hi, n), 1)
            keep = jnp.where((col >= lo) & (col < hi), 0.0, m[hi:, :])
            m[hi:, :] = keep - dot3(r[:, hi:], r, TN)
            col = lax.broadcasted_iota(jnp.int32, (b, n), 1)
            r = jnp.where(col < hi, r, 0.0)
        m[lo:hi, :] = r


def reduce_kernel(
    slab, sketch_map,
    sketch_t, gram_out, cross_out,
    slab_v, map_v, map_t, skf, skh, gacc, gpack, gsib, gpart, gred, gline, gtot,
    cross, from_core, from_a, from_b, line,
    load_sem, map_sem, out_sem,
    g0s, g0r, g1s, g1r, g2s, g2r, g3s, g3r,
    cas, car, cbs, cbr, ccs, ccr, cds, cdr, ces, cer,
):
    g = lax.axis_index("grp")
    d = lax.axis_index("dev")
    y, c = g // 2, g % 2
    z, x = d // SIDE, d % SIDE
    other = g + 1 - 2 * c
    ma = z + c * (x - z)
    mb = x + c * (z - x)
    sa = SIDE - c * (SIDE - 1)
    sb = 1 + c * (SIDE - 1)
    lane_c = pl.multiple_of(c * HALF, 8)
    lane_o = pl.multiple_of((1 - c) * HALF, 8)

    map_copy = pltpu.make_async_copy(sketch_map, map_v, map_sem)
    map_copy.start()

    def load(i):
        rows = pl.ds(pl.multiple_of(i * CHUNK, CHUNK), CHUNK)
        return pltpu.make_async_copy(slab.at[rows, :], slab_v.at[rows, :], load_sem.at[i])

    for i in range(LOCAL // CHUNK):
        load(i).start()

    barrier = pltpu.get_barrier_semaphore()

    def greet(i, carry):
        to = lax.rem(d + i, SLICES)
        pl.semaphore_signal(barrier, inc=1, device_id=(g, to), device_id_type=MESH)
        pl.semaphore_signal(barrier, inc=1, device_id=(other, to), device_id_type=MESH)
        return carry

    lax.fori_loop(1, SLICES, greet, 0)
    pl.semaphore_signal(barrier, inc=1, device_id=(other, d), device_id_type=MESH)
    for i in range(1, SIDE):
        to = lax.rem(y + i, SIDE) * 2 + c
        pl.semaphore_signal(barrier, inc=1, device_id=(to, d), device_id_type=MESH)

    map_copy.wait()
    for i in range(N // CHUNK):
        map_t[:, i * CHUNK : (i + 1) * CHUNK] = map_v[i * CHUNK : (i + 1) * CHUNK, :].T
    gacc[...] = jnp.zeros_like(gacc)

    def sketch_chunk(i, carry):
        load(i).wait()
        rows = pl.ds(pl.multiple_of(i * CHUNK, CHUNK), CHUNK)
        s = dot(map_t[...], slab_v[rows, :], NT)
        skf[:, rows] = s
        high, low = split(s)
        skh[:, rows] = high
        gacc[...] += dot(high, high, NT) + (dot(high, low, NT) + dot(low, high, NT))
        return carry

    lax.fori_loop(0, LOCAL // CHUNK, sketch_chunk, 0)
    sketch_out = pltpu.make_async_copy(skf, sketch_t, out_sem)
    sketch_out.start()

    zero = jnp.zeros((16, 8, 128), F32)
    gpack[0:16] = gacc[0:128, 0:128].reshape(16, 8, 128)
    gpack[16:32] = gacc[0:128, 128:256].reshape(16, 8, 128)
    gpack[32:48] = zero
    gpack[32:48, :, 0:64] = gacc[0:128, 256:320].reshape(16, 8, 64)
    gpack[48:64] = gacc[128:256, 128:256].reshape(16, 8, 128)
    gpack[64:80] = zero
    gpack[64:80, :, 0:64] = gacc[128:256, 256:320].reshape(16, 8, 64)
    gpack[80:96] = zero
    gpack[80:88, :, 0:64] = gacc[256:320, 256:320].reshape(8, 8, 64)

    pl.semaphore_wait(barrier, 2 * (SLICES - 1) + 1 + SIDE - 1)

    def remote(src, dst, send, recv, to_g, to_d):
        return pltpu.make_async_remote_copy(
            src_ref=src, dst_ref=dst, send_sem=send, recv_sem=recv,
            device_id=(to_g, to_d), device_id_type=MESH,
        )

    def place(core, s):
        return jnp.where(core == 0, s, (s % SIDE) * SIDE + s // SIDE)

    def core_copy(s):
        return remote(
            cross.at[place(c, s), pl.ds(lane_o, HALF), :], from_core.at[place(1 - c, s)],
            cas.at[s], car.at[s], other, d,
        )

    def cross_block(t, carry):
        both = dot(skh[...], slab_v[:, pl.ds(pl.multiple_of(t * 2 * WIDTH, 2 * WIDTH), 2 * WIDTH)], NN)
        cross[place(c, 2 * t)] = both[:, :WIDTH]
        cross[place(c, 2 * t + 1)] = both[:, WIDTH:]
        core_copy(2 * t).start()
        core_copy(2 * t + 1).start()
        return carry

    def run_cross(first, last):
        lax.fori_loop(first, last, cross_block, 0)

    g0 = remote(gpack, gsib, g0s, g0r, other, d)
    g0.start()
    run_cross(0, 2)
    g0.wait()
    gpart[...] = gpack[...] + gsib[...]

    def g1(i):
        to = lax.rem(d + i, SLICES)
        first = c * (TILES // 2) + to * PIECE
        return remote(gpart.at[pl.ds(first, PIECE)], gred.at[i], g1s.at[i], g1r.at[i], g, to)

    def start(copy):
        def body(i, carry):
            copy(i).start()
            return carry
        return body

    def wait(copy):
        def body(i, carry):
            copy(i).wait()
            return carry
        return body

    lax.fori_loop(1, SLICES, start(g1), 0)
    run_cross(2, 5)
    lax.fori_loop(1, SLICES, wait(g1), 0)
    mine = c * (TILES // 2) + d * PIECE
    total = gpart[pl.ds(mine, PIECE)]
    for i in range(1, SLICES):
        total = total + gred[i]
    gline[pl.ds(y, 1)] = total[None]

    def g2(i):
        to = lax.rem(y + i, SIDE) * 2 + c
        return remote(gline.at[y], gline.at[y], g2s.at[i], g2r.at[i], to, d)

    lax.fori_loop(1, SIDE, start(g2), 0)
    run_cross(5, 6)
    lax.fori_loop(1, SIDE, wait(g2), 0)
    gtot[pl.ds(mine, PIECE)] = (gline[0] + gline[1]) + (gline[2] + gline[3])

    def g3(i):
        k, to = i // SLICES, lax.rem(d + i, SLICES)
        return remote(
            gtot.at[pl.ds(mine, PIECE)], gtot.at[pl.ds(mine, PIECE)],
            g3s.at[i], g3r.at[i], g + k * (other - g), to,
        )

    lax.fori_loop(1, 2 * SLICES, start(g3), 0)
    run_cross(6, 8)

    lax.fori_loop(0, SLICES, wait(core_copy), 0)

    def add_core(p):
        cross[p, pl.ds(lane_c, HALF), :] += from_core[p]

    def ca(i):
        to = lax.rem(ma + i, SIDE)
        return remote(
            cross.at[pl.ds(to * SIDE, SIDE), pl.ds(lane_c, HALF), :], from_a.at[i],
            cas.at[SLICES + i], car.at[SLICES + i], g, to * sa + mb * sb,
        )

    def ca_start(i, carry):
        to = lax.rem(ma + i, SIDE)
        for j in range(SIDE):
            add_core(to * SIDE + j)
        ca(i).start()
        return carry

    lax.fori_loop(1, SIDE, ca_start, 0)
    for j in range(SIDE):
        add_core(ma * SIDE + j)

    lax.fori_loop(1, 2 * SLICES, wait(g3), 0)
    gram_out[...] = jnp.zeros_like(gram_out)
    gram_out[0:128, 0:128] = gtot[0:16].reshape(128, 128)
    gram_out[0:128, 128:256] = gtot[16:32].reshape(128, 128)
    gram_out[0:128, 256:320] = gtot[32:48, :, 0:64].reshape(128, 64)
    gram_out[128:256, 128:256] = gtot[48:64].reshape(128, 128)
    gram_out[128:256, 256:320] = gtot[64:80, :, 0:64].reshape(128, 64)
    gram_out[256:320, 256:320] = gtot[80:88, :, 0:64].reshape(64, 64)

    lax.fori_loop(1, SIDE, wait(ca), 0)

    def add_a(j):
        p = ma * SIDE + j
        cross[p, pl.ds(lane_c, HALF), :] += (from_a[1, j] + from_a[2, j]) + from_a[3, j]

    def cb(i):
        to = lax.rem(mb + i, SIDE)
        return remote(
            cross.at[ma * SIDE + to, pl.ds(lane_c, HALF), :], from_b.at[i],
            cbs.at[i], cbr.at[i], g, ma * sa + to * sb,
        )

    def cb_start(i, carry):
        add_a(lax.rem(mb + i, SIDE))
        cb(i).start()
        return carry

    lax.fori_loop(1, SIDE, cb_start, 0)
    add_a(mb)
    lax.fori_loop(1, SIDE, wait(cb), 0)
    line[pl.ds(y, 1)] = (
        (cross[ma * SIDE + mb, pl.ds(lane_c, HALF), :] + from_b[1]) + (from_b[2] + from_b[3])
    )[None]

    def cc(i):
        to = lax.rem(y + i, SIDE) * 2 + c
        return remote(line.at[y], line.at[y], ccs.at[i], ccr.at[i], to, d)

    lax.fori_loop(1, SIDE, start(cc), 0)
    lax.fori_loop(1, SIDE, wait(cc), 0)
    cross_out[pl.ds(lane_c, HALF), :] = (line[0] + line[1]) + (line[2] + line[3])

    rows = pl.ds(lane_c, HALF)
    last = remote(cross_out.at[rows, :], cross_out.at[rows, :], ces, cer, other, d)
    last.start()
    last.wait()
    sketch_out.wait()


def reduce_call(slab, sketch_map):
    dma = pltpu.SemaphoreType.DMA
    return pl.pallas_call(
        reduce_kernel,
        out_shape=(
            jax.ShapeDtypeStruct((SK, LOCAL), F32),
            jax.ShapeDtypeStruct((SK, SK), F32),
            jax.ShapeDtypeStruct((SK, WIDTH), F32),
        ),
        in_specs=[pl.BlockSpec(memory_space=pl.ANY)] * 2,
        out_specs=(
            pl.BlockSpec(memory_space=pl.ANY),
            pl.BlockSpec(memory_space=pltpu.VMEM),
            pl.BlockSpec(memory_space=pltpu.VMEM),
        ),
        scratch_shapes=[
            pltpu.VMEM((LOCAL, N), BF16),
            pltpu.VMEM((N, SK), BF16),
            pltpu.VMEM((SK, N), BF16),
            pltpu.VMEM((SK, LOCAL), F32),
            pltpu.VMEM((SK, LOCAL), BF16),
            pltpu.VMEM((SK, SK), F32),
            pltpu.VMEM((TILES, 8, 128), F32),
            pltpu.VMEM((TILES, 8, 128), F32),
            pltpu.VMEM((TILES, 8, 128), F32),
            pltpu.VMEM((SLICES, PIECE, 8, 128), F32),
            pltpu.VMEM((SIDE, PIECE, 8, 128), F32),
            pltpu.VMEM((TILES, 8, 128), F32),
            pltpu.VMEM((SLICES, SK, WIDTH), F32),
            pltpu.VMEM((SLICES, HALF, WIDTH), F32),
            pltpu.VMEM((SIDE, SIDE, HALF, WIDTH), F32),
            pltpu.VMEM((SIDE, HALF, WIDTH), F32),
            pltpu.VMEM((SIDE, HALF, WIDTH), F32),
            dma((LOCAL // CHUNK,)), dma, dma,
            dma, dma,
            dma((SLICES,)), dma((SLICES,)),
            dma((SIDE,)), dma((SIDE,)),
            dma((2 * SLICES,)), dma((2 * SLICES,)),
            dma((SLICES + SIDE,)), dma((SLICES + SIDE,)),
            dma((SIDE,)), dma((SIDE,)),
            dma((SIDE,)), dma((SIDE,)),
            dma((SIDE,)), dma((SIDE,)),
            dma, dma,
        ],
        compiler_params=pltpu.CompilerParams(
            collective_id=0, has_side_effects=True, vmem_limit_bytes=58 << 20
        ),
        cost_estimate=pl.CostEstimate(
            flops=4 * LOCAL * N * SK, bytes_accessed=24 << 20, transcendentals=0
        ),
        name="sketch_and_sums",
    )(slab, sketch_map)


def finish_kernel(scale, gram, cross, sketch_t, basis, coeffs, m, skf, out, load_sem, out_sem):
    load = pltpu.make_async_copy(sketch_t, skf, load_sem)
    load.start()
    m[...] = gram[...]
    invert_factor(m, SK, 64, 16)
    coeffs[...] = dot3(m[...], cross[...], NN) * (1.0 / scale)
    high, low = split(m[...] * scale)
    load.wait()

    def store(i):
        rows = pl.ds(i * CHUNK, CHUNK)
        return pltpu.make_async_copy(out.at[rows, :], basis.at[rows, :], out_sem.at[i])

    for i in range(LOCAL // CHUNK):
        sh, sl = split(skf[:, i * CHUNK : (i + 1) * CHUNK])
        b = dot(high, sh, NN) + (dot(high, sl, NN) + dot(low, sh, NN))
        out[i * CHUNK : (i + 1) * CHUNK, :] = b.T
        store(i).start()
    for i in range(LOCAL // CHUNK):
        store(i).wait()


def finish_call(scale, gram, cross, sketch_t):
    def kernel(*refs):
        finish_kernel(scale, *refs)

    vmem = pl.BlockSpec(memory_space=pltpu.VMEM)
    hbm = pl.BlockSpec(memory_space=pl.ANY)
    return pl.pallas_call(
        kernel,
        out_shape=(
            jax.ShapeDtypeStruct((LOCAL, SK), F32),
            jax.ShapeDtypeStruct((SK, WIDTH), F32),
        ),
        in_specs=[vmem, vmem, hbm],
        out_specs=(hbm, vmem),
        scratch_shapes=[
            pltpu.VMEM((SK, SK), F32),
            pltpu.VMEM((SK, LOCAL), F32),
            pltpu.VMEM((LOCAL, SK), F32),
            pltpu.SemaphoreType.DMA,
            pltpu.SemaphoreType.DMA((LOCAL // CHUNK,)),
        ],
        compiler_params=pltpu.CompilerParams(vmem_limit_bytes=48 << 20),
        name="factor_and_basis",
    )(gram, cross, sketch_t)


def local(slab, sketch_map):
    rows = slab.shape[0] * lax.axis_size("grp") * lax.axis_size("dev")
    scale = math.sqrt(rows)
    sketch_t, gram, cross = reduce_call(slab, sketch_map)
    return finish_call(scale, gram, cross, sketch_t)


def solution(mesh):
    in_specs = (P(("grp", "dev"), None), P())
    out_specs = (P(("grp", "dev"), None), P(None, "dev"))
    return jax.shard_map(local, mesh=mesh, in_specs=in_specs, out_specs=out_specs, check_vma=False)
```

```python
import math

import jax
import jax.numpy as jnp
from jax import lax
from jax.experimental import pallas as pl
from jax.experimental.pallas import tpu as pltpu
from jax.sharding import PartitionSpec as P

F32 = jnp.float32
BF16 = jnp.bfloat16
NN = (((1,), (0,)), ((), ()))
NT = (((1,), (1,)), ((), ()))
TN = (((0,), (0,)), ((), ()))
MESH = pl.DeviceIdType.MESH

N = 4096
SK = 320
HALF = SK // 2
LOCAL = 2048
CHUNK = 512
WIDTH = 256
SLICES = 16
SIDE = 4


def dot(a, b, dims):
    return lax.dot_general(a, b, dims, preferred_element_type=F32)


def split(a):
    high = a.astype(BF16)
    return high, (a - high.astype(F32)).astype(BF16)


def dot3(a, b, dims):
    ah, al = split(a)
    bh, bl = split(b)
    return dot(ah, bh, dims) + (dot(ah, bl, dims) + dot(al, bh, dims))


def factor_block(a, n, w):
    eye = lax.broadcasted_iota(jnp.int32, (n, n), 0) == lax.broadcasted_iota(jnp.int32, (n, n), 1)
    m = jnp.concatenate([a, eye.astype(F32)], axis=1)
    width = 2 * n
    row_in_group = lax.broadcasted_iota(jnp.int32, (8, width), 0)
    per = w // 8
    groups = [m[8 * g : 8 * g + 8] for g in range(n // 8)]
    done = []
    for p in range(n // w):
        rows = groups[p * per : (p + 1) * per]
        cols = [
            [jnp.broadcast_to(r[:, p * w + l : p * w + l + 1], (8, width)) for r in rows]
            for l in range(w)
        ]
        pivots = [jnp.ones((8, width), F32) for _ in rows]
        for k in range(w):
            g, i = divmod(k, 8)
            pivot = jnp.broadcast_to(cols[k][g][i : i + 1], (8, width))
            inverse = 1.0 / pivot
            factor = {}
            for h in range(g, per):
                factor[h] = cols[k][h] * inverse
            factor[g] = jnp.where(row_in_group > i, factor[g], 0.0)
            for l in range(k + 1, w):
                value = jnp.broadcast_to(cols[l][g][i : i + 1], (8, width))
                for h in range(g, per):
                    cols[l][h] = cols[l][h] - factor[h] * value
            value = jnp.broadcast_to(rows[g][i : i + 1], (8, width))
            for h in range(g, per):
                rows[h] = rows[h] - factor[h] * value
            pivots[g] = jnp.where(row_in_group == i, pivot, pivots[g])
        block = jnp.concatenate([r * lax.rsqrt(v) for r, v in zip(rows, pivots)], axis=0)
        done.append(block[:, n:])
        if p < n // w - 1:
            high, low = split(block)
            left = jnp.concatenate([high, low, high], axis=0)[:, :n]
            right = jnp.concatenate([high, high, low], axis=0)
            update = dot(left, right, TN)
            for g in range((p + 1) * per, n // 8):
                groups[g] = groups[g] - update[8 * g : 8 * g + 8]
    return jnp.concatenate(done, axis=0)


def invert_step(m, k, n, b, w):
    lo, hi = k * b, (k + 1) * b
    t = factor_block(m[lo:hi, lo:hi], b, w)
    r = dot3(t, m[lo:hi, :], NN)
    parts = [r[:, :lo]] if lo else []
    parts.append(t)
    if hi < n:
        parts.append(r[:, hi:])
    r = jnp.concatenate(parts, axis=1)
    if hi < n:
        col = lax.broadcasted_iota(jnp.int32, (n - hi, n), 1)
        keep = jnp.where((col >= lo) & (col < hi), 0.0, m[hi:, :])
        m[hi:, :] = keep - dot3(r[:, hi:], r, TN)
        col = lax.broadcasted_iota(jnp.int32, (b, n), 1)
        r = jnp.where(col < hi, r, 0.0)
    m[lo:hi, :] = r


DIST = (0, 1, 2, 1)
AROUND = sorted(
    ((i, j) for i in range(SIDE) for j in range(SIDE) if (i, j) != (0, 0)),
    key=lambda p: -(DIST[p[0]] + DIST[p[1]]),
)
CELLS = (
    [(2, j) for j in range(4)] + [(0, 2), (1, 2), (3, 2)]
    + [(1, 0), (1, 1), (1, 3), (0, 1), (3, 1)]
    + [(3, 0), (3, 3), (0, 3)]
    + [(0, 0)]
)
BLOCK = 64
EVEN = [(i, j) for j in (0, 2, 4) for i in range(j + 1)]
ODD = [(i, j) for j in (1, 3) for i in range(j + 1)]
PACK = [(i, j, n, 0) for n, (i, j) in enumerate(EVEN[:8])]
PACK += [(i, j, n, 1) for n, (i, j) in enumerate(ODD + EVEN[8:])]
TILES = 64
PIECE = TILES // 32
PART = HALF // SIDE


def table(q, values):
    return sum(jnp.where(q == k, v, 0) for k, v in enumerate(values) if v)


def reduce_kernel(
    slab, map_rows,
    sketch_t, m, cross_out,
    slab_v, map_t, skf, skh, skl, gpack, gsib, gred, gline, gtot,
    cross, from_core, from_a, from_b, line, from_y,
    load_sem, map_sem, out_sem,
    g0s, g0r, g1s, g1r, g2s, g2r, g3s, g3r, g4s, g4r,
    xs, xr, as_, ar, bs, br, ys, yr, zs, zr,
):
    g = lax.axis_index("grp")
    d = lax.axis_index("dev")
    y, c = g // 2, g % 2
    z, x = d // SIDE, d % SIDE
    other = g + 1 - 2 * c
    row_c = pl.multiple_of(c * HALF, 8)
    row_o = pl.multiple_of((1 - c) * HALF, 8)
    mine = pl.ds(row_c, HALF)

    map_copy = pltpu.make_async_copy(map_rows, map_t, map_sem)
    map_copy.start()

    def load(i):
        rows = pl.ds(pl.multiple_of(i * CHUNK, CHUNK), CHUNK)
        return pltpu.make_async_copy(slab.at[rows, :], slab_v.at[rows, :], load_sem.at[i])

    load(0).start()
    load(1).start()

    def chip(dz, dx):
        return lax.rem(z + dz, SIDE) * SIDE + lax.rem(x + dx, SIDE)

    def along_a(i):
        return jnp.where(c == 0, chip(i, 0), chip(0, i))

    def along_b(i):
        return jnp.where(c == 0, chip(0, i), chip(i, 0))

    def along_y(i, core):
        return lax.rem(y + i, SIDE) * 2 + core

    barrier = pltpu.get_barrier_semaphore()

    def greet(to_g, to_d):
        pl.semaphore_signal(barrier, inc=1, device_id=(to_g, to_d), device_id_type=MESH)

    for dz, dx in AROUND:
        greet(g, chip(dz, dx))
    for i in range(1, SIDE):
        greet(along_y(i, c), d)
    for i in range(SIDE):
        greet(along_y(i, 1 - c), d)

    map_copy.wait()

    def sketch_chunk(i, carry):
        load(i).wait()

        @pl.when(i + 2 < LOCAL // CHUNK)
        def _():
            load(i + 2).start()

        rows = pl.ds(pl.multiple_of(i * CHUNK, CHUNK), CHUNK)
        s = dot(map_t[...], slab_v[rows, :], NT)
        skf[:, rows] = s
        high, low = split(s)
        skh[:, rows] = high
        skl[:, rows] = low
        return carry

    lax.fori_loop(0, LOCAL // CHUNK, sketch_chunk, 0)
    sketch_out = pltpu.make_async_copy(skf, sketch_t, out_sem)
    sketch_out.start()

    mixed = dot(skl[...], skh[...], NT)
    gram = dot(skh[...], skh[...], NT) + (mixed + mixed.T)
    gpack[56:64] = jnp.zeros((8, 8, 128), F32)
    for i, j, n, h in PACK:
        block = gram[i * BLOCK : (i + 1) * BLOCK, j * BLOCK : (j + 1) * BLOCK]
        gpack[8 * n : 8 * n + 8, :, h * BLOCK : (h + 1) * BLOCK] = block.reshape(8, 8, BLOCK)

    pl.semaphore_wait(barrier, len(AROUND) + 2 * SIDE - 1)

    def remote(src, dst, send, recv, to_g, to_d):
        return pltpu.make_async_remote_copy(
            src_ref=src, dst_ref=dst, send_sem=send, recv_sem=recv,
            device_id=(to_g, to_d), device_id_type=MESH,
        )

    def core_copy(q):
        dz, dx = table(q, [p[0] for p in CELLS]), table(q, [p[1] for p in CELLS])
        here = jnp.where(c == 0, dz * SIDE + dx, dx * SIDE + dz)
        there = jnp.where(c == 0, dx * SIDE + dz, dz * SIDE + dx)
        return remote(
            cross.at[here, pl.ds(row_o, HALF), :], from_core.at[there],
            xs.at[q], xr.at[q], other, d,
        )

    def cross_cell(q, carry):
        dz, dx = table(q, [p[0] for p in CELLS]), table(q, [p[1] for p in CELLS])
        here = jnp.where(c == 0, dz * SIDE + dx, dx * SIDE + dz)
        columns = pl.ds(pl.multiple_of(chip(dz, dx) * WIDTH, WIDTH), WIDTH)
        cross[here] = dot(skh[...], slab_v[:, columns], NN)
        core_copy(q).start()
        return carry

    def run_cross(first, last):
        lax.fori_loop(first, last, cross_cell, 0)

    def cross_arrived(first, last):
        def body(q, carry):
            core_copy(q).wait()
            return carry
        lax.fori_loop(first, last, body, 0)

    def add_core(p):
        cross[p, mine, :] += from_core[p]

    g0 = remote(gpack, gsib, g0s, g0r, other, d)
    g0.start()
    run_cross(0, 3)
    g0.wait()
    gsib[...] = gpack[...] + gsib[...]

    def g1(dz, dx):
        to = chip(dz, dx)
        k = dz * SIDE + dx
        part = pl.ds(c * (TILES // 2) + to * PIECE, PIECE)
        return remote(gsib.at[part], gred.at[k], g1s.at[k], g1r.at[k], g, to)

    for p in AROUND:
        g1(*p).start()
    run_cross(3, 8)

    def a_copy(k):
        first = (8, 10, 6, 12, 4, 14)[k]
        to = along_a(1 if k % 2 == 0 else SIDE - 1)
        return remote(
            cross.at[pl.ds(first, 2), mine, :], from_a.at[k], as_.at[k], ar.at[k], g, to
        )

    cross_arrived(0, 7)
    for p in range(8, 12):
        add_core(p)
    a_copy(0).start()
    a_copy(1).start()
    run_cross(8, 16)

    for p in AROUND[::-1]:
        g1(*p).wait()
    part = pl.ds(c * (TILES // 2) + d * PIECE, PIECE)
    total = gsib[part]
    for dz, dx in AROUND:
        total = total + gred[dz * SIDE + dx]
    gline[pl.ds(y, 1)] = total[None]

    def g2(i):
        return remote(gline.at[y], gline.at[y], g2s.at[i], g2r.at[i], along_y(i, c), d)

    for i in (2, 1, 3):
        g2(i).start()

    cross_arrived(7, 16)
    for p in (4, 5, 6, 7, 12, 13, 14, 15):
        add_core(p)
    a_copy(2).start()
    a_copy(3).start()
    for p in range(4):
        add_core(p)

    for i in (1, 3, 2):
        g2(i).wait()
    gtot[part] = (gline[0] + gline[1]) + (gline[2] + gline[3])

    def g3(dz, dx):
        k = dz * SIDE + dx
        return remote(gtot.at[part], gtot.at[part], g3s.at[k], g3r.at[k], g, chip(dz, dx))

    for p in AROUND:
        g3(*p).start()

    a_copy(0).wait()
    a_copy(1).wait()
    cross[4:6, mine, :] += from_a[0]
    cross[14:16, mine, :] += from_a[1]
    a_copy(4).start()
    a_copy(5).start()

    for p in AROUND[::-1]:
        g3(*p).wait()
    half = pl.ds(c * (TILES // 2), TILES // 2)
    g4 = remote(gtot.at[half], gtot.at[half], g4s, g4r, other, d)
    g4.start()
    m[...] = jnp.zeros_like(m)
    g4.wait()
    for i, j, n, h in PACK:
        block = gtot[8 * n : 8 * n + 8, :, h * BLOCK : (h + 1) * BLOCK].reshape(BLOCK, BLOCK)
        m[i * BLOCK : (i + 1) * BLOCK, j * BLOCK : (j + 1) * BLOCK] = block

    def factor_step(k):
        invert_step(m, k, SK, BLOCK, 16)

    factor_step(0)

    for k in range(2, 6):
        a_copy(k).wait()
    cross[0:2, mine, :] += from_a[4] + from_a[3]
    cross[2:4, mine, :] += from_a[2] + from_a[5]

    def b_copy(i):
        return remote(cross.at[i, mine, :], from_b.at[i], bs.at[i], br.at[i], g, along_b(i))

    for i in (2, 1, 3):
        b_copy(i).start()
    factor_step(1)
    for i in (1, 3, 2):
        b_copy(i).wait()
    line[...] = (cross[0, mine, :] + from_b[1]) + (from_b[2] + from_b[3])

    def y_copy(i):
        rows = pl.ds(pl.multiple_of(lax.rem(y + i, SIDE) * PART, 8), PART)
        return remote(line.at[rows, :], from_y.at[i], ys.at[i], yr.at[i], along_y(i, c), d)

    for i in (2, 1, 3):
        y_copy(i).start()
    factor_step(2)
    for i in (1, 3, 2):
        y_copy(i).wait()
    own = line[pl.ds(pl.multiple_of(y * PART, 8), PART), :]
    final = pl.ds(pl.multiple_of(c * HALF + y * PART, 8), PART)
    cross_out[final, :] = (own + from_y[1]) + (from_y[2] + from_y[3])

    def z_copy(k):
        i, flip = k % SIDE, k // SIDE
        core = c + flip * (1 - 2 * c)
        return remote(
            cross_out.at[final, :], cross_out.at[final, :], zs.at[k], zr.at[k],
            along_y(i, core), d,
        )

    for k in range(1, 2 * SIDE):
        z_copy(k).start()
    factor_step(3)
    factor_step(4)
    for k in range(1, 2 * SIDE):
        z_copy(k).wait()
    sketch_out.wait()


def reduce_call(slab, map_rows):
    dma = pltpu.SemaphoreType.DMA
    return pl.pallas_call(
        reduce_kernel,
        out_shape=(
            jax.ShapeDtypeStruct((SK, LOCAL), F32),
            jax.ShapeDtypeStruct((SK, SK), F32),
            jax.ShapeDtypeStruct((SK, WIDTH), F32),
        ),
        in_specs=[pl.BlockSpec(memory_space=pl.ANY)] * 2,
        out_specs=(
            pl.BlockSpec(memory_space=pl.ANY),
            pl.BlockSpec(memory_space=pltpu.VMEM),
            pl.BlockSpec(memory_space=pltpu.VMEM),
        ),
        scratch_shapes=[
            pltpu.VMEM((LOCAL, N), BF16),
            pltpu.VMEM((SK, N), BF16),
            pltpu.VMEM((SK, LOCAL), F32),
            pltpu.VMEM((SK, LOCAL), BF16),
            pltpu.VMEM((SK, LOCAL), BF16),
            pltpu.VMEM((TILES, 8, 128), F32),
            pltpu.VMEM((TILES, 8, 128), F32),
            pltpu.VMEM((SLICES, PIECE, 8, 128), F32),
            pltpu.VMEM((SIDE, PIECE, 8, 128), F32),
            pltpu.VMEM((TILES, 8, 128), F32),
            pltpu.VMEM((SLICES, SK, WIDTH), F32),
            pltpu.VMEM((SLICES, HALF, WIDTH), F32),
            pltpu.VMEM((6, 2, HALF, WIDTH), F32),
            pltpu.VMEM((SIDE, HALF, WIDTH), F32),
            pltpu.VMEM((HALF, WIDTH), F32),
            pltpu.VMEM((SIDE, PART, WIDTH), F32),
            dma((LOCAL // CHUNK,)), dma, dma,
            dma, dma,
            dma((SLICES,)), dma((SLICES,)),
            dma((SIDE,)), dma((SIDE,)),
            dma((SLICES,)), dma((SLICES,)),
            dma, dma,
            dma((SLICES,)), dma((SLICES,)),
            dma((6,)), dma((6,)),
            dma((SIDE,)), dma((SIDE,)),
            dma((SIDE,)), dma((SIDE,)),
            dma((2 * SIDE,)), dma((2 * SIDE,)),
        ],
        compiler_params=pltpu.CompilerParams(
            collective_id=0, has_side_effects=True, vmem_limit_bytes=58 << 20
        ),
        cost_estimate=pl.CostEstimate(
            flops=4 * LOCAL * N * SK, bytes_accessed=24 << 20, transcendentals=0
        ),
        name="sketch_and_sums",
    )(slab, map_rows)


def finish_kernel(scale, inverse, cross, sketch_t, basis_t, coeffs, m, cr, skf, out, m_sem, cross_sem, load_sem, out_sem):
    m_copy = pltpu.make_async_copy(inverse, m, m_sem)
    m_copy.start()
    cross_copy = pltpu.make_async_copy(cross, cr, cross_sem)
    cross_copy.start()
    load = pltpu.make_async_copy(sketch_t, skf, load_sem)
    load.start()
    m_copy.wait()
    high, low = split(m[...] * scale)
    load.wait()

    def store(i):
        part = pl.ds(i * CHUNK, CHUNK)
        return pltpu.make_async_copy(out.at[:, part], basis_t.at[:, part], out_sem.at[i])

    for i in range(LOCAL // CHUNK):
        part = slice(i * CHUNK, (i + 1) * CHUNK)
        sh, sl = split(skf[:, part])
        out[:, part] = dot(high, sh, NN) + (dot(high, sl, NN) + dot(low, sh, NN))
        store(i).start()
    cross_copy.wait()
    coeffs[...] = dot3(m[...], cr[...], NN) * (1.0 / scale)
    for i in range(LOCAL // CHUNK):
        store(i).wait()


def finish_call(scale, inverse, cross, sketch_t):
    def kernel(*refs):
        finish_kernel(scale, *refs)

    vmem = pl.BlockSpec(memory_space=pltpu.VMEM)
    hbm = pl.BlockSpec(memory_space=pl.ANY)
    dma = pltpu.SemaphoreType.DMA
    return pl.pallas_call(
        kernel,
        out_shape=(
            jax.ShapeDtypeStruct((SK, LOCAL), F32),
            jax.ShapeDtypeStruct((SK, WIDTH), F32),
        ),
        in_specs=[hbm, hbm, hbm],
        out_specs=(hbm, vmem),
        scratch_shapes=[
            pltpu.VMEM((SK, SK), F32),
            pltpu.VMEM((SK, WIDTH), F32),
            pltpu.VMEM((SK, LOCAL), F32),
            pltpu.VMEM((SK, LOCAL), F32),
            dma, dma, dma,
            dma((LOCAL // CHUNK,)),
        ],
        compiler_params=pltpu.CompilerParams(vmem_limit_bytes=60 << 20),
        name="basis_and_coeffs",
    )(inverse, cross, sketch_t)


def local(slab, sketch_map):
    rows = slab.shape[0] * lax.axis_size("grp") * lax.axis_size("dev")
    scale = math.sqrt(rows)
    sketch_t, inverse, cross = reduce_call(slab, sketch_map.T)
    basis_t, coeffs = finish_call(scale, inverse, cross, sketch_t)
    return basis_t.T, coeffs


def solution(mesh):
    in_specs = (P(("grp", "dev"), None), P())
    out_specs = (P(("grp", "dev"), None), P(None, "dev"))
    return jax.shard_map(local, mesh=mesh, in_specs=in_specs, out_specs=out_specs, check_vma=False)
```

```python
import math

import jax
import jax.numpy as jnp
from jax import lax
from jax.experimental import pallas as pl
from jax.experimental.pallas import tpu as pltpu
from jax.sharding import PartitionSpec as P

F32 = jnp.float32
BF16 = jnp.bfloat16
NN = (((1,), (0,)), ((), ()))
NT = (((1,), (1,)), ((), ()))
TN = (((0,), (0,)), ((), ()))
MESH = pl.DeviceIdType.MESH

N = 4096
SK = 320
HALF = SK // 2
LOCAL = 2048
CHUNK = 512
WIDTH = 256
SLICES = 16
SIDE = 4


def dot(a, b, dims):
    return lax.dot_general(a, b, dims, preferred_element_type=F32)


def split(a):
    high = a.astype(BF16)
    return high, (a - high.astype(F32)).astype(BF16)


def dot3(a, b, dims):
    ah, al = split(a)
    bh, bl = split(b)
    return dot(ah, bh, dims) + (dot(ah, bl, dims) + dot(al, bh, dims))


def factor_block(a, n, w):
    eye = lax.broadcasted_iota(jnp.int32, (n, n), 0) == lax.broadcasted_iota(jnp.int32, (n, n), 1)
    m = jnp.concatenate([a, eye.astype(F32)], axis=1)
    width = 2 * n
    row_in_group = lax.broadcasted_iota(jnp.int32, (8, width), 0)
    per = w // 8
    groups = [m[8 * g : 8 * g + 8] for g in range(n // 8)]
    done = []
    for p in range(n // w):
        rows = groups[p * per : (p + 1) * per]
        cols = [
            [jnp.broadcast_to(r[:, p * w + l : p * w + l + 1], (8, width)) for r in rows]
            for l in range(w)
        ]
        pivots = [jnp.ones((8, width), F32) for _ in rows]
        for k in range(w):
            g, i = divmod(k, 8)
            pivot = jnp.broadcast_to(cols[k][g][i : i + 1], (8, width))
            inverse = 1.0 / pivot
            factor = {}
            for h in range(g, per):
                factor[h] = cols[k][h] * inverse
            factor[g] = jnp.where(row_in_group > i, factor[g], 0.0)
            for l in range(k + 1, w):
                value = jnp.broadcast_to(cols[l][g][i : i + 1], (8, width))
                for h in range(g, per):
                    cols[l][h] = cols[l][h] - factor[h] * value
            value = jnp.broadcast_to(rows[g][i : i + 1], (8, width))
            for h in range(g, per):
                rows[h] = rows[h] - factor[h] * value
            pivots[g] = jnp.where(row_in_group == i, pivot, pivots[g])
        block = jnp.concatenate([r * lax.rsqrt(v) for r, v in zip(rows, pivots)], axis=0)
        done.append(block[:, n:])
        if p < n // w - 1:
            high, low = split(block)
            left = jnp.concatenate([high, low, high], axis=0)[:, :n]
            right = jnp.concatenate([high, high, low], axis=0)
            update = dot(left, right, TN)
            for g in range((p + 1) * per, n // 8):
                groups[g] = groups[g] - update[8 * g : 8 * g + 8]
    return jnp.concatenate(done, axis=0)


def invert_step(m, k, n, b, w):
    lo, hi = k * b, (k + 1) * b
    t = factor_block(m[lo:hi, lo:hi], b, w)
    r = dot3(t, m[lo:hi, :], NN)
    parts = [r[:, :lo]] if lo else []
    parts.append(t)
    if hi < n:
        parts.append(r[:, hi:])
    r = jnp.concatenate(parts, axis=1)
    if hi < n:
        col = lax.broadcasted_iota(jnp.int32, (n - hi, n), 1)
        keep = jnp.where((col >= lo) & (col < hi), 0.0, m[hi:, :])
        m[hi:, :] = keep - dot3(r[:, hi:], r, TN)
        col = lax.broadcasted_iota(jnp.int32, (b, n), 1)
        r = jnp.where(col < hi, r, 0.0)
    m[lo:hi, :] = r


DIST = (0, 1, 2, 1)
AROUND = sorted(
    ((i, j) for i in range(SIDE) for j in range(SIDE) if (i, j) != (0, 0)),
    key=lambda p: -(DIST[p[0]] + DIST[p[1]]),
)
CELLS = (
    [(2, j) for j in range(4)] + [(0, 2), (1, 2), (3, 2)]
    + [(1, 0), (1, 1), (1, 3), (0, 1), (3, 1)]
    + [(3, 0), (3, 3), (0, 3)]
    + [(0, 0)]
)
BLOCK = 64
EVEN = [(i, j) for j in (0, 2, 4) for i in range(j + 1)]
ODD = [(i, j) for j in (1, 3) for i in range(j + 1)]
PACK = [(i, j, n, 0) for n, (i, j) in enumerate(EVEN[:8])]
PACK += [(i, j, n, 1) for n, (i, j) in enumerate(ODD + EVEN[8:])]
TILES = 64
PIECE = TILES // 32
PART = HALF // SIDE


def table(q, values):
    return sum(jnp.where(q == k, v, 0) for k, v in enumerate(values) if v)


def reduce_kernel(
    slab, map_rows,
    sketch_t, m, cross_out,
    slab_v, map_t, parts, gpack, gsib, gred, gline, gtot,
    cross, from_core, from_a, from_b, line, from_y,
    load_sem, map_sem, out_sem,
    g0s, g0r, g1s, g1r, g2s, g2r, g3s, g3r, g4s, g4r,
    xs, xr, as_, ar, bs, br, ys, yr, zs, zr,
):
    g = lax.axis_index("grp")
    d = lax.axis_index("dev")
    y, c = g // 2, g % 2
    z, x = d // SIDE, d % SIDE
    other = g + 1 - 2 * c
    row_c = pl.multiple_of(c * HALF, 8)
    row_o = pl.multiple_of((1 - c) * HALF, 8)
    mine = pl.ds(row_c, HALF)

    map_copy = pltpu.make_async_copy(map_rows, map_t, map_sem)
    map_copy.start()

    def load(i):
        rows = pl.ds(pl.multiple_of(i * CHUNK, CHUNK), CHUNK)
        return pltpu.make_async_copy(slab.at[rows, :], slab_v.at[rows, :], load_sem.at[i])

    load(0).start()
    load(1).start()

    def chip(dz, dx):
        return lax.rem(z + dz, SIDE) * SIDE + lax.rem(x + dx, SIDE)

    def along_a(i):
        return jnp.where(c == 0, chip(i, 0), chip(0, i))

    def along_b(i):
        return jnp.where(c == 0, chip(0, i), chip(i, 0))

    def along_y(i, core):
        return lax.rem(y + i, SIDE) * 2 + core

    barrier = pltpu.get_barrier_semaphore()

    def greet(to_g, to_d):
        pl.semaphore_signal(barrier, inc=1, device_id=(to_g, to_d), device_id_type=MESH)

    for dz, dx in AROUND:
        greet(g, chip(dz, dx))
    for i in range(1, SIDE):
        greet(along_y(i, c), d)
    for i in range(SIDE):
        greet(along_y(i, 1 - c), d)

    map_copy.wait()

    def sketch_chunk(i, carry):
        load(i).wait()

        @pl.when(i + 2 < LOCAL // CHUNK)
        def _():
            load(i + 2).start()

        rows = pl.ds(pl.multiple_of(i * CHUNK, CHUNK), CHUNK)
        s = dot(map_t[...], slab_v[rows, :], NT)
        high, low = split(s)
        parts[:SK, rows] = high
        parts[SK:, rows] = low
        return carry

    lax.fori_loop(0, LOCAL // CHUNK, sketch_chunk, 0)
    sketch_out = pltpu.make_async_copy(parts, sketch_t, out_sem)
    sketch_out.start()

    mixed = dot(parts[SK:], parts[:SK], NT)
    gram = dot(parts[:SK], parts[:SK], NT) + (mixed + mixed.T)
    gpack[56:64] = jnp.zeros((8, 8, 128), F32)
    for i, j, n, h in PACK:
        block = gram[i * BLOCK : (i + 1) * BLOCK, j * BLOCK : (j + 1) * BLOCK]
        gpack[8 * n : 8 * n + 8, :, h * BLOCK : (h + 1) * BLOCK] = block.reshape(8, 8, BLOCK)

    pl.semaphore_wait(barrier, len(AROUND) + 2 * SIDE - 1)

    def remote(src, dst, send, recv, to_g, to_d):
        return pltpu.make_async_remote_copy(
            src_ref=src, dst_ref=dst, send_sem=send, recv_sem=recv,
            device_id=(to_g, to_d), device_id_type=MESH,
        )

    def core_copy(q):
        dz, dx = table(q, [p[0] for p in CELLS]), table(q, [p[1] for p in CELLS])
        here = jnp.where(c == 0, dz * SIDE + dx, dx * SIDE + dz)
        there = jnp.where(c == 0, dx * SIDE + dz, dz * SIDE + dx)
        return remote(
            cross.at[here, pl.ds(row_o, HALF), :], from_core.at[there],
            xs.at[q], xr.at[q], other, d,
        )

    def cross_cell(q, carry):
        dz, dx = table(q, [p[0] for p in CELLS]), table(q, [p[1] for p in CELLS])
        here = jnp.where(c == 0, dz * SIDE + dx, dx * SIDE + dz)
        columns = pl.ds(pl.multiple_of(chip(dz, dx) * WIDTH, WIDTH), WIDTH)
        cross[here] = dot(parts[:SK], slab_v[:, columns], NN)
        core_copy(q).start()
        return carry

    def run_cross(first, last):
        lax.fori_loop(first, last, cross_cell, 0)

    def cross_arrived(first, last):
        def body(q, carry):
            core_copy(q).wait()
            return carry
        lax.fori_loop(first, last, body, 0)

    def add_core(p):
        cross[p, mine, :] += from_core[p]

    g0 = remote(gpack, gsib, g0s, g0r, other, d)
    g0.start()
    run_cross(0, 3)
    g0.wait()
    gsib[...] = gpack[...] + gsib[...]

    def g1(dz, dx):
        to = chip(dz, dx)
        k = dz * SIDE + dx
        part = pl.ds(c * (TILES // 2) + to * PIECE, PIECE)
        return remote(gsib.at[part], gred.at[k], g1s.at[k], g1r.at[k], g, to)

    for p in AROUND:
        g1(*p).start()
    run_cross(3, 7)

    def a_copy(k):
        first = (8, 10, 6, 12, 4, 14)[k]
        to = along_a(1 if k % 2 == 0 else SIDE - 1)
        return remote(
            cross.at[pl.ds(first, 2), mine, :], from_a.at[k], as_.at[k], ar.at[k], g, to
        )

    cross_arrived(0, 7)
    for p in range(8, 12):
        add_core(p)
    a_copy(0).start()
    a_copy(1).start()
    run_cross(7, 12)
    cross_arrived(7, 12)
    for p in range(4, 8):
        add_core(p)
    a_copy(2).start()
    run_cross(12, 16)
    cross_arrived(12, 15)
    for p in range(12, 16):
        add_core(p)
    a_copy(3).start()

    for p in AROUND[::-1]:
        g1(*p).wait()
    part = pl.ds(c * (TILES // 2) + d * PIECE, PIECE)
    total = gsib[part]
    for dz, dx in AROUND:
        total = total + gred[dz * SIDE + dx]
    gline[pl.ds(y, 1)] = total[None]

    def g2(i):
        return remote(gline.at[y], gline.at[y], g2s.at[i], g2r.at[i], along_y(i, c), d)

    for i in (2, 1, 3):
        g2(i).start()

    a_copy(0).wait()
    a_copy(1).wait()
    cross[4:6, mine, :] += from_a[0]
    cross[14:16, mine, :] += from_a[1]
    a_copy(4).start()
    a_copy(5).start()
    cross_arrived(15, 16)
    for p in range(4):
        add_core(p)

    for i in (1, 3, 2):
        g2(i).wait()
    gtot[part] = (gline[0] + gline[1]) + (gline[2] + gline[3])

    def g3(dz, dx):
        k = dz * SIDE + dx
        return remote(gtot.at[part], gtot.at[part], g3s.at[k], g3r.at[k], g, chip(dz, dx))

    for p in AROUND:
        g3(*p).start()

    for k in range(2, 6):
        a_copy(k).wait()
    cross[0:2, mine, :] += from_a[4] + from_a[3]
    cross[2:4, mine, :] += from_a[2] + from_a[5]

    def b_copy(i):
        return remote(cross.at[i, mine, :], from_b.at[i], bs.at[i], br.at[i], g, along_b(i))

    for i in (2, 1, 3):
        b_copy(i).start()

    for p in AROUND[::-1]:
        g3(*p).wait()
    half = pl.ds(c * (TILES // 2), TILES // 2)
    g4 = remote(gtot.at[half], gtot.at[half], g4s, g4r, other, d)
    g4.start()
    m[...] = jnp.zeros_like(m)
    g4.wait()
    for i, j, n, h in PACK:
        block = gtot[8 * n : 8 * n + 8, :, h * BLOCK : (h + 1) * BLOCK].reshape(BLOCK, BLOCK)
        m[i * BLOCK : (i + 1) * BLOCK, j * BLOCK : (j + 1) * BLOCK] = block

    def factor_step(k):
        invert_step(m, k, SK, BLOCK, 16)

    for i in (1, 3, 2):
        b_copy(i).wait()
    line[...] = (cross[0, mine, :] + from_b[1]) + (from_b[2] + from_b[3])

    def y_copy(i):
        rows = pl.ds(pl.multiple_of(lax.rem(y + i, SIDE) * PART, 8), PART)
        return remote(line.at[rows, :], from_y.at[i], ys.at[i], yr.at[i], along_y(i, c), d)

    for i in (2, 1, 3):
        y_copy(i).start()
    factor_step(0)
    factor_step(1)
    for i in (1, 3, 2):
        y_copy(i).wait()
    own = line[pl.ds(pl.multiple_of(y * PART, 8), PART), :]
    final = pl.ds(pl.multiple_of(c * HALF + y * PART, 8), PART)
    cross_out[final, :] = (own + from_y[1]) + (from_y[2] + from_y[3])

    def z_copy(k):
        i, flip = k % SIDE, k // SIDE
        core = c + flip * (1 - 2 * c)
        return remote(
            cross_out.at[final, :], cross_out.at[final, :], zs.at[k], zr.at[k],
            along_y(i, core), d,
        )

    for k in range(1, 2 * SIDE):
        z_copy(k).start()
    factor_step(2)
    factor_step(3)
    factor_step(4)
    for k in range(1, 2 * SIDE):
        z_copy(k).wait()
    sketch_out.wait()


def reduce_call(slab, map_rows):
    dma = pltpu.SemaphoreType.DMA
    return pl.pallas_call(
        reduce_kernel,
        out_shape=(
            jax.ShapeDtypeStruct((2 * SK, LOCAL), BF16),
            jax.ShapeDtypeStruct((SK, SK), F32),
            jax.ShapeDtypeStruct((SK, WIDTH), F32),
        ),
        in_specs=[pl.BlockSpec(memory_space=pl.ANY)] * 2,
        out_specs=(
            pl.BlockSpec(memory_space=pl.ANY),
            pl.BlockSpec(memory_space=pltpu.VMEM),
            pl.BlockSpec(memory_space=pltpu.VMEM),
        ),
        scratch_shapes=[
            pltpu.VMEM((LOCAL, N), BF16),
            pltpu.VMEM((SK, N), BF16),
            pltpu.VMEM((2 * SK, LOCAL), BF16),
            pltpu.VMEM((TILES, 8, 128), F32),
            pltpu.VMEM((TILES, 8, 128), F32),
            pltpu.VMEM((SLICES, PIECE, 8, 128), F32),
            pltpu.VMEM((SIDE, PIECE, 8, 128), F32),
            pltpu.VMEM((TILES, 8, 128), F32),
            pltpu.VMEM((SLICES, SK, WIDTH), F32),
            pltpu.VMEM((SLICES, HALF, WIDTH), F32),
            pltpu.VMEM((6, 2, HALF, WIDTH), F32),
            pltpu.VMEM((SIDE, HALF, WIDTH), F32),
            pltpu.VMEM((HALF, WIDTH), F32),
            pltpu.VMEM((SIDE, PART, WIDTH), F32),
            dma((LOCAL // CHUNK,)), dma, dma,
            dma, dma,
            dma((SLICES,)), dma((SLICES,)),
            dma((SIDE,)), dma((SIDE,)),
            dma((SLICES,)), dma((SLICES,)),
            dma, dma,
            dma((SLICES,)), dma((SLICES,)),
            dma((6,)), dma((6,)),
            dma((SIDE,)), dma((SIDE,)),
            dma((SIDE,)), dma((SIDE,)),
            dma((2 * SIDE,)), dma((2 * SIDE,)),
        ],
        compiler_params=pltpu.CompilerParams(
            collective_id=0, has_side_effects=True, vmem_limit_bytes=58 << 20
        ),
        cost_estimate=pl.CostEstimate(
            flops=4 * LOCAL * N * SK, bytes_accessed=24 << 20, transcendentals=0
        ),
        name="sketch_and_sums",
    )(slab, map_rows)


def finish_kernel(
    scale, inverse, cross, sketch_t, basis_t, coeffs, m, cr, parts, out, m_sem, cross_sem, load_sem, out_sem
):
    m_copy = pltpu.make_async_copy(inverse, m, m_sem)
    m_copy.start()

    def load(i):
        part = pl.ds(pl.multiple_of(i * CHUNK, CHUNK), CHUNK)
        return pltpu.make_async_copy(sketch_t.at[:, part], parts.at[:, part], load_sem.at[i])

    for i in range(LOCAL // CHUNK):
        load(i).start()
    cross_copy = pltpu.make_async_copy(cross, cr, cross_sem)
    cross_copy.start()
    m_copy.wait()
    high, low = split(m[...] * scale)
    left = jnp.concatenate([high, high, low], axis=1)

    def store(i):
        part = pl.ds(pl.multiple_of(i * CHUNK, CHUNK), CHUNK)
        return pltpu.make_async_copy(out.at[:, part], basis_t.at[:, part], out_sem.at[i])

    for i in range(LOCAL // CHUNK):
        part = pl.ds(i * CHUNK, CHUNK)
        load(i).wait()
        right = jnp.concatenate([parts[:, part], parts[:SK, part]], axis=0)
        out[:, part] = dot(left, right, NN)
        store(i).start()
    cross_copy.wait()
    coeffs[...] = dot3(m[...], cr[...], NN) * (1.0 / scale)
    for i in range(LOCAL // CHUNK):
        store(i).wait()


def finish_call(scale, inverse, cross, sketch_t):
    def kernel(*refs):
        finish_kernel(scale, *refs)

    vmem = pl.BlockSpec(memory_space=pltpu.VMEM)
    hbm = pl.BlockSpec(memory_space=pl.ANY)
    dma = pltpu.SemaphoreType.DMA
    return pl.pallas_call(
        kernel,
        out_shape=(
            jax.ShapeDtypeStruct((SK, LOCAL), F32),
            jax.ShapeDtypeStruct((SK, WIDTH), F32),
        ),
        in_specs=[hbm, hbm, hbm],
        out_specs=(hbm, vmem),
        scratch_shapes=[
            pltpu.VMEM((SK, SK), F32),
            pltpu.VMEM((SK, WIDTH), F32),
            pltpu.VMEM((2 * SK, LOCAL), BF16),
            pltpu.VMEM((SK, LOCAL), F32),
            dma, dma,
            dma((LOCAL // CHUNK,)), dma((LOCAL // CHUNK,)),
        ],
        compiler_params=pltpu.CompilerParams(vmem_limit_bytes=60 << 20),
        name="basis_and_coeffs",
    )(inverse, cross, sketch_t)


def local(slab, sketch_map):
    rows = slab.shape[0] * lax.axis_size("grp") * lax.axis_size("dev")
    scale = math.sqrt(rows)
    sketch_t, inverse, cross = reduce_call(slab, sketch_map.T)
    basis_t, coeffs = finish_call(scale, inverse, cross, sketch_t)
    return basis_t.T, coeffs


def solution(mesh):
    in_specs = (P(("grp", "dev"), None), P())
    out_specs = (P(("grp", "dev"), None), P(None, "dev"))
    return jax.shard_map(local, mesh=mesh, in_specs=in_specs, out_specs=out_specs, check_vma=False)
```

```python
import math

import jax
import jax.numpy as jnp
from jax import lax
from jax.experimental import pallas as pl
from jax.experimental.pallas import tpu as pltpu
from jax.sharding import PartitionSpec as P

F32 = jnp.float32
BF16 = jnp.bfloat16
NN = (((1,), (0,)), ((), ()))
NT = (((1,), (1,)), ((), ()))
TN = (((0,), (0,)), ((), ()))
MESH = pl.DeviceIdType.MESH

N = 4096
SK = 320
HALF = SK // 2
LOCAL = 2048
CHUNK = 512
WIDTH = 256
SLICES = 16
SIDE = 4


def dot(a, b, dims):
    return lax.dot_general(a, b, dims, preferred_element_type=F32)


def split(a):
    high = a.astype(BF16)
    return high, (a - high.astype(F32)).astype(BF16)


def dot3(a, b, dims):
    ah, al = split(a)
    bh, bl = split(b)
    return dot(ah, bh, dims) + (dot(ah, bl, dims) + dot(al, bh, dims))


def factor_block(a, n, w):
    eye = lax.broadcasted_iota(jnp.int32, (n, n), 0) == lax.broadcasted_iota(jnp.int32, (n, n), 1)
    m = jnp.concatenate([a, eye.astype(F32)], axis=1)
    width = 2 * n
    row_in_group = lax.broadcasted_iota(jnp.int32, (8, width), 0)
    per = w // 8
    groups = [m[8 * g : 8 * g + 8] for g in range(n // 8)]
    done = []

    def spread(value, i):
        return jnp.broadcast_to(value[i : i + 1], (8, width))

    for p in range(n // w):
        rows = groups[p * per :]
        cols = [
            [jnp.broadcast_to(r[:, p * w + l : p * w + l + 1], (8, width)) for r in rows]
            for l in range(w)
        ]
        pivots = [jnp.ones((8, width), F32) for _ in range(per)]
        for k in range(w):
            g, i = divmod(k, 8)
            pivot = spread(cols[k][g], i)
            inverse = 1.0 / pivot
            left = range(g, len(rows))
            factor = {h: cols[k][h] * inverse for h in left}
            factor[g] = jnp.where(row_in_group > i, factor[g], 0.0)
            for l in range(k + 1, w):
                value = spread(cols[l][g], i)
                for h in left:
                    cols[l][h] = cols[l][h] - factor[h] * value
            value = spread(rows[g], i)
            for h in left:
                rows[h] = rows[h] - factor[h] * value
            pivots[g] = jnp.where(row_in_group == i, pivot, pivots[g])
        for h in range(per):
            done.append((rows[h] * lax.rsqrt(pivots[h]))[:, n:])
        groups[p * per :] = rows
    return jnp.concatenate(done, axis=0)


def invert_step(m, k, n, b, w):
    lo, hi = k * b, (k + 1) * b
    t = factor_block(m[lo:hi, lo:hi], b, w)
    r = dot3(t, m[lo:hi, :], NN)
    parts = [r[:, :lo]] if lo else []
    parts.append(t)
    if hi < n:
        parts.append(r[:, hi:])
    r = jnp.concatenate(parts, axis=1)
    if hi < n:
        col = lax.broadcasted_iota(jnp.int32, (n - hi, n), 1)
        keep = jnp.where((col >= lo) & (col < hi), 0.0, m[hi:, :])
        m[hi:, :] = keep - dot3(r[:, hi:], r, TN)
        col = lax.broadcasted_iota(jnp.int32, (b, n), 1)
        r = jnp.where(col < hi, r, 0.0)
    m[lo:hi, :] = r


DIST = (0, 1, 2, 1)
AROUND = sorted(
    ((i, j) for i in range(SIDE) for j in range(SIDE) if (i, j) != (0, 0)),
    key=lambda p: -(DIST[p[0]] + DIST[p[1]]),
)
CELLS = (
    [(2, j) for j in range(4)] + [(0, 2), (1, 2), (3, 2)]
    + [(1, 0), (1, 1), (1, 3), (0, 1), (3, 1)]
    + [(3, 0), (3, 3), (0, 3)]
    + [(0, 0)]
)
BLOCK = 64
EVEN = [(i, j) for j in (0, 2, 4) for i in range(j + 1)]
ODD = [(i, j) for j in (1, 3) for i in range(j + 1)]
PACK = [(i, j, n, 0) for n, (i, j) in enumerate(EVEN[:8])]
PACK += [(i, j, n, 1) for n, (i, j) in enumerate(ODD + EVEN[8:])]
TILES = 64
PIECE = TILES // 32
PART = HALF // SIDE


def table(q, values):
    return sum(jnp.where(q == k, v, 0) for k, v in enumerate(values) if v)


def reduce_kernel(
    slab, map_rows,
    sketch_t, m, cross_out,
    slab_v, map_t, parts, gpack, gsib, gred, gline, gtot,
    cross, from_core, from_a, from_b, line, from_y,
    load_sem, map_sem, out_sem,
    g0s, g0r, g1s, g1r, g2s, g2r, g3s, g3r,
    xs, xr, as_, ar, bs, br, ys, yr, zs, zr,
):
    g = lax.axis_index("grp")
    d = lax.axis_index("dev")
    y, c = g // 2, g % 2
    z, x = d // SIDE, d % SIDE
    other = g + 1 - 2 * c
    row_c = pl.multiple_of(c * HALF, 8)
    row_o = pl.multiple_of((1 - c) * HALF, 8)
    mine = pl.ds(row_c, HALF)

    map_copy = pltpu.make_async_copy(map_rows, map_t, map_sem)
    map_copy.start()

    def load(i):
        rows = pl.ds(pl.multiple_of(i * CHUNK, CHUNK), CHUNK)
        return pltpu.make_async_copy(slab.at[rows, :], slab_v.at[rows, :], load_sem.at[i])

    load(0).start()
    load(1).start()

    def chip(dz, dx):
        return lax.rem(z + dz, SIDE) * SIDE + lax.rem(x + dx, SIDE)

    def along_a(i):
        return jnp.where(c == 0, chip(i, 0), chip(0, i))

    def along_b(i):
        return jnp.where(c == 0, chip(0, i), chip(i, 0))

    def along_y(i, core):
        return lax.rem(y + i, SIDE) * 2 + core

    barrier = pltpu.get_barrier_semaphore()

    def greet(to_g, to_d):
        pl.semaphore_signal(barrier, inc=1, device_id=(to_g, to_d), device_id_type=MESH)

    for dz, dx in AROUND:
        greet(g, chip(dz, dx))
        greet(other, chip(dz, dx))
    for i in range(1, SIDE):
        greet(along_y(i, c), d)
    for i in range(SIDE):
        greet(along_y(i, 1 - c), d)

    map_copy.wait()

    def sketch_chunk(i, carry):
        load(i).wait()

        @pl.when(i + 2 < LOCAL // CHUNK)
        def _():
            load(i + 2).start()

        rows = pl.ds(pl.multiple_of(i * CHUNK, CHUNK), CHUNK)
        s = dot(map_t[...], slab_v[rows, :], NT)
        high, low = split(s)
        parts[:SK, rows] = high
        parts[SK:, rows] = low
        return carry

    lax.fori_loop(0, LOCAL // CHUNK, sketch_chunk, 0)
    sketch_out = pltpu.make_async_copy(parts, sketch_t, out_sem)
    sketch_out.start()

    mixed = dot(parts[SK:], parts[:SK], NT)
    gram = dot(parts[:SK], parts[:SK], NT) + (mixed + mixed.T)
    gpack[56:64] = jnp.zeros((8, 8, 128), F32)
    for i, j, n, h in PACK:
        block = gram[i * BLOCK : (i + 1) * BLOCK, j * BLOCK : (j + 1) * BLOCK]
        gpack[8 * n : 8 * n + 8, :, h * BLOCK : (h + 1) * BLOCK] = block.reshape(8, 8, BLOCK)

    pl.semaphore_wait(barrier, 2 * len(AROUND) + 2 * SIDE - 1)

    def remote(src, dst, send, recv, to_g, to_d):
        return pltpu.make_async_remote_copy(
            src_ref=src, dst_ref=dst, send_sem=send, recv_sem=recv,
            device_id=(to_g, to_d), device_id_type=MESH,
        )

    def core_copy(q):
        dz, dx = table(q, [p[0] for p in CELLS]), table(q, [p[1] for p in CELLS])
        here = jnp.where(c == 0, dz * SIDE + dx, dx * SIDE + dz)
        there = jnp.where(c == 0, dx * SIDE + dz, dz * SIDE + dx)
        return remote(
            cross.at[here, pl.ds(row_o, HALF), :], from_core.at[there],
            xs.at[q], xr.at[q], other, d,
        )

    def cross_cell(q):
        dz, dx = table(q, [p[0] for p in CELLS]), table(q, [p[1] for p in CELLS])
        here = jnp.where(c == 0, dz * SIDE + dx, dx * SIDE + dz)
        columns = pl.ds(pl.multiple_of(chip(dz, dx) * WIDTH, WIDTH), WIDTH)
        return here, dot(parts[:SK], slab_v[:, columns], NN)

    def cross_pair(t, carry):
        first, a = cross_cell(2 * t)
        second, b = cross_cell(2 * t + 1)
        cross[first] = a
        cross[second] = b
        core_copy(2 * t).start()
        core_copy(2 * t + 1).start()
        return carry

    def run_cross(first, last):
        lax.fori_loop(first // 2, last // 2, cross_pair, 0)

    def cross_arrived(first, last):
        def body(q, carry):
            core_copy(q).wait()
            return carry
        lax.fori_loop(first, last, body, 0)

    def add_core(p):
        cross[p, mine, :] += from_core[p]

    g0 = remote(gpack, gsib, g0s, g0r, other, d)
    g0.start()
    run_cross(0, 4)
    g0.wait()
    gsib[...] = gpack[...] + gsib[...]

    def g1(dz, dx):
        to = chip(dz, dx)
        k = dz * SIDE + dx
        part = pl.ds(c * (TILES // 2) + to * PIECE, PIECE)
        return remote(gsib.at[part], gred.at[k], g1s.at[k], g1r.at[k], g, to)

    for p in AROUND:
        g1(*p).start()
    run_cross(4, 8)

    def a_copy(k):
        first = (8, 10, 6, 12, 4, 14)[k]
        to = along_a(1 if k % 2 == 0 else SIDE - 1)
        return remote(
            cross.at[pl.ds(first, 2), mine, :], from_a.at[k], as_.at[k], ar.at[k], g, to
        )

    cross_arrived(0, 7)
    for p in range(8, 12):
        add_core(p)
    a_copy(0).start()
    a_copy(1).start()
    run_cross(8, 12)
    cross_arrived(7, 12)
    for p in range(4, 8):
        add_core(p)
    a_copy(2).start()
    run_cross(12, 16)
    cross_arrived(12, 15)
    for p in range(12, 16):
        add_core(p)
    a_copy(3).start()

    for p in AROUND[::-1]:
        g1(*p).wait()
    part = pl.ds(c * (TILES // 2) + d * PIECE, PIECE)
    total = gsib[part]
    for dz, dx in AROUND:
        total = total + gred[dz * SIDE + dx]
    gline[pl.ds(y, 1)] = total[None]

    def g2(i):
        return remote(gline.at[y], gline.at[y], g2s.at[i], g2r.at[i], along_y(i, c), d)

    for i in (2, 1, 3):
        g2(i).start()

    a_copy(0).wait()
    a_copy(1).wait()
    cross[4:6, mine, :] += from_a[0]
    cross[14:16, mine, :] += from_a[1]
    a_copy(4).start()
    a_copy(5).start()
    cross_arrived(15, 16)
    for p in range(4):
        add_core(p)

    for i in (1, 3, 2):
        g2(i).wait()
    gtot[part] = (gline[0] + gline[1]) + (gline[2] + gline[3])

    def g3(flip, dz, dx):
        k = flip * SLICES + dz * SIDE + dx
        to_g = other if flip else g
        return remote(gtot.at[part], gtot.at[part], g3s.at[k], g3r.at[k], to_g, chip(dz, dx))

    handed = [(flip, dz, dx) for dz, dx in AROUND for flip in (0, 1)] + [(1, 0, 0)]
    for p in handed:
        g3(*p).start()

    for k in range(2, 6):
        a_copy(k).wait()
    cross[0:2, mine, :] += from_a[4] + from_a[3]
    cross[2:4, mine, :] += from_a[2] + from_a[5]

    def b_copy(i):
        return remote(cross.at[i, mine, :], from_b.at[i], bs.at[i], br.at[i], g, along_b(i))

    for i in (2, 1, 3):
        b_copy(i).start()

    m[...] = jnp.zeros_like(m)
    for p in handed[::-1]:
        g3(*p).wait()
    for i, j, n, h in PACK:
        block = gtot[8 * n : 8 * n + 8, :, h * BLOCK : (h + 1) * BLOCK].reshape(BLOCK, BLOCK)
        m[i * BLOCK : (i + 1) * BLOCK, j * BLOCK : (j + 1) * BLOCK] = block

    def factor_step(k):
        invert_step(m, k, SK, BLOCK, 16)

    for i in (1, 3, 2):
        b_copy(i).wait()
    line[...] = (cross[0, mine, :] + from_b[1]) + (from_b[2] + from_b[3])

    def y_copy(i):
        rows = pl.ds(pl.multiple_of(lax.rem(y + i, SIDE) * PART, 8), PART)
        return remote(line.at[rows, :], from_y.at[i], ys.at[i], yr.at[i], along_y(i, c), d)

    for i in (2, 1, 3):
        y_copy(i).start()
    factor_step(0)
    factor_step(1)
    for i in (1, 3, 2):
        y_copy(i).wait()
    own = line[pl.ds(pl.multiple_of(y * PART, 8), PART), :]
    final = pl.ds(pl.multiple_of(c * HALF + y * PART, 8), PART)
    cross_out[final, :] = (own + from_y[1]) + (from_y[2] + from_y[3])

    def z_copy(k):
        i, flip = k % SIDE, k // SIDE
        core = c + flip * (1 - 2 * c)
        return remote(
            cross_out.at[final, :], cross_out.at[final, :], zs.at[k], zr.at[k],
            along_y(i, core), d,
        )

    for k in range(1, 2 * SIDE):
        z_copy(k).start()
    factor_step(2)
    factor_step(3)
    factor_step(4)
    for k in range(1, 2 * SIDE):
        z_copy(k).wait()
    sketch_out.wait()


def reduce_call(slab, map_rows):
    dma = pltpu.SemaphoreType.DMA
    return pl.pallas_call(
        reduce_kernel,
        out_shape=(
            jax.ShapeDtypeStruct((2 * SK, LOCAL), BF16),
            jax.ShapeDtypeStruct((SK, SK), F32),
            jax.ShapeDtypeStruct((SK, WIDTH), F32),
        ),
        in_specs=[pl.BlockSpec(memory_space=pl.ANY)] * 2,
        out_specs=(
            pl.BlockSpec(memory_space=pl.ANY),
            pl.BlockSpec(memory_space=pltpu.VMEM),
            pl.BlockSpec(memory_space=pltpu.VMEM),
        ),
        scratch_shapes=[
            pltpu.VMEM((LOCAL, N), BF16),
            pltpu.VMEM((SK, N), BF16),
            pltpu.VMEM((2 * SK, LOCAL), BF16),
            pltpu.VMEM((TILES, 8, 128), F32),
            pltpu.VMEM((TILES, 8, 128), F32),
            pltpu.VMEM((SLICES, PIECE, 8, 128), F32),
            pltpu.VMEM((SIDE, PIECE, 8, 128), F32),
            pltpu.VMEM((TILES, 8, 128), F32),
            pltpu.VMEM((SLICES, SK, WIDTH), F32),
            pltpu.VMEM((SLICES, HALF, WIDTH), F32),
            pltpu.VMEM((6, 2, HALF, WIDTH), F32),
            pltpu.VMEM((SIDE, HALF, WIDTH), F32),
            pltpu.VMEM((HALF, WIDTH), F32),
            pltpu.VMEM((SIDE, PART, WIDTH), F32),
            dma((LOCAL // CHUNK,)), dma, dma,
            dma, dma,
            dma((SLICES,)), dma((SLICES,)),
            dma((SIDE,)), dma((SIDE,)),
            dma((2 * SLICES,)), dma((2 * SLICES,)),
            dma((SLICES,)), dma((SLICES,)),
            dma((6,)), dma((6,)),
            dma((SIDE,)), dma((SIDE,)),
            dma((SIDE,)), dma((SIDE,)),
            dma((2 * SIDE,)), dma((2 * SIDE,)),
        ],
        compiler_params=pltpu.CompilerParams(
            collective_id=0, has_side_effects=True, vmem_limit_bytes=58 << 20
        ),
        cost_estimate=pl.CostEstimate(
            flops=4 * LOCAL * N * SK, bytes_accessed=24 << 20, transcendentals=0
        ),
        name="sketch_and_sums",
    )(slab, map_rows)


def finish_kernel(
    scale, inverse, cross, sketch_t, basis_t, coeffs, m, cr, parts, out, m_sem, cross_sem, load_sem, out_sem
):
    m_copy = pltpu.make_async_copy(inverse, m, m_sem)
    m_copy.start()

    def load(i):
        part = pl.ds(pl.multiple_of(i * CHUNK, CHUNK), CHUNK)
        return pltpu.make_async_copy(sketch_t.at[:, part], parts.at[:, part], load_sem.at[i])

    for i in range(LOCAL // CHUNK):
        load(i).start()
    cross_copy = pltpu.make_async_copy(cross, cr, cross_sem)
    cross_copy.start()
    m_copy.wait()
    high, low = split(m[...] * scale)
    left = jnp.concatenate([high, high, low], axis=1)

    def store(i):
        part = pl.ds(pl.multiple_of(i * CHUNK, CHUNK), CHUNK)
        return pltpu.make_async_copy(out.at[:, part], basis_t.at[:, part], out_sem.at[i])

    for i in range(LOCAL // CHUNK):
        part = pl.ds(i * CHUNK, CHUNK)
        load(i).wait()
        right = jnp.concatenate([parts[:, part], parts[:SK, part]], axis=0)
        out[:, part] = dot(left, right, NN)
        store(i).start()
    cross_copy.wait()
    coeffs[...] = dot3(m[...], cr[...], NN) * (1.0 / scale)
    for i in range(LOCAL // CHUNK):
        store(i).wait()


def finish_call(scale, inverse, cross, sketch_t):
    def kernel(*refs):
        finish_kernel(scale, *refs)

    vmem = pl.BlockSpec(memory_space=pltpu.VMEM)
    hbm = pl.BlockSpec(memory_space=pl.ANY)
    dma = pltpu.SemaphoreType.DMA
    return pl.pallas_call(
        kernel,
        out_shape=(
            jax.ShapeDtypeStruct((SK, LOCAL), F32),
            jax.ShapeDtypeStruct((SK, WIDTH), F32),
        ),
        in_specs=[hbm, hbm, hbm],
        out_specs=(hbm, vmem),
        scratch_shapes=[
            pltpu.VMEM((SK, SK), F32),
            pltpu.VMEM((SK, WIDTH), F32),
            pltpu.VMEM((2 * SK, LOCAL), BF16),
            pltpu.VMEM((SK, LOCAL), F32),
            dma, dma,
            dma((LOCAL // CHUNK,)), dma((LOCAL // CHUNK,)),
        ],
        compiler_params=pltpu.CompilerParams(vmem_limit_bytes=60 << 20),
        name="basis_and_coeffs",
    )(inverse, cross, sketch_t)


def local(slab, sketch_map):
    rows = slab.shape[0] * lax.axis_size("grp") * lax.axis_size("dev")
    scale = math.sqrt(rows)
    sketch_t, inverse, cross = reduce_call(slab, sketch_map.T)
    basis_t, coeffs = finish_call(scale, inverse, cross, sketch_t)
    return basis_t.T, coeffs


def solution(mesh):
    in_specs = (P(("grp", "dev"), None), P())
    out_specs = (P(("grp", "dev"), None), P(None, "dev"))
    return jax.shard_map(local, mesh=mesh, in_specs=in_specs, out_specs=out_specs, check_vma=False)
```

```python
import math

import jax
import jax.numpy as jnp
from jax import lax
from jax.experimental import pallas as pl
from jax.experimental.pallas import tpu as pltpu
from jax.sharding import PartitionSpec as P

F32 = jnp.float32
BF16 = jnp.bfloat16
NN = (((1,), (0,)), ((), ()))
NT = (((1,), (1,)), ((), ()))
TN = (((0,), (0,)), ((), ()))
MESH = pl.DeviceIdType.MESH

N = 4096
SK = 320
HALF = SK // 2
LOCAL = 2048
CHUNK = 512
STEP = 1024
WIDTH = 256
SLICES = 16
SIDE = 4


def dot(a, b, dims):
    return lax.dot_general(a, b, dims, preferred_element_type=F32)


def split(a):
    high = a.astype(BF16)
    return high, (a - high.astype(F32)).astype(BF16)


def dot3(a, b, dims):
    ah, al = split(a)
    bh, bl = split(b)
    return dot(ah, bh, dims) + (dot(ah, bl, dims) + dot(al, bh, dims))


def factor_block(a, n, w):
    eye = lax.broadcasted_iota(jnp.int32, (n, n), 0) == lax.broadcasted_iota(jnp.int32, (n, n), 1)
    m = jnp.concatenate([a, eye.astype(F32)], axis=1)
    width = 2 * n
    row_in_group = lax.broadcasted_iota(jnp.int32, (8, width), 0)
    per = w // 8
    groups = [m[8 * g : 8 * g + 8] for g in range(n // 8)]
    done = []

    def spread(value, i):
        return jnp.broadcast_to(value[i : i + 1], (8, width))

    for p in range(n // w):
        rows = groups[p * per :]
        cols = [
            [jnp.broadcast_to(r[:, p * w + l : p * w + l + 1], (8, width)) for r in rows]
            for l in range(w)
        ]
        pivots = [jnp.ones((8, width), F32) for _ in range(per)]
        for k in range(w):
            g, i = divmod(k, 8)
            pivot = spread(cols[k][g], i)
            inverse = 1.0 / pivot
            left = range(g, len(rows))
            factor = {h: cols[k][h] * inverse for h in left}
            factor[g] = jnp.where(row_in_group > i, factor[g], 0.0)
            for l in range(k + 1, w):
                value = spread(cols[l][g], i)
                for h in left:
                    cols[l][h] = cols[l][h] - factor[h] * value
            value = spread(rows[g], i)
            for h in left:
                rows[h] = rows[h] - factor[h] * value
            pivots[g] = jnp.where(row_in_group == i, pivot, pivots[g])
        for h in range(per):
            done.append((rows[h] * lax.rsqrt(pivots[h]))[:, n:])
        groups[p * per :] = rows
    return jnp.concatenate(done, axis=0)


def invert_step(m, k, n, b, w):
    lo, hi = k * b, (k + 1) * b
    t = factor_block(m[lo:hi, lo:hi], b, w)
    r = dot3(t, m[lo:hi, :], NN)
    parts = [r[:, :lo]] if lo else []
    parts.append(t)
    if hi < n:
        parts.append(r[:, hi:])
    r = jnp.concatenate(parts, axis=1)
    if hi < n:
        col = lax.broadcasted_iota(jnp.int32, (n - hi, n), 1)
        keep = jnp.where((col >= lo) & (col < hi), 0.0, m[hi:, :])
        m[hi:, :] = keep - dot3(r[:, hi:], r, TN)
        col = lax.broadcasted_iota(jnp.int32, (b, n), 1)
        r = jnp.where(col < hi, r, 0.0)
    m[lo:hi, :] = r


DIST = (0, 1, 2, 1)
AROUND = sorted(
    ((i, j) for i in range(SIDE) for j in range(SIDE) if (i, j) != (0, 0)),
    key=lambda p: -(DIST[p[0]] + DIST[p[1]]),
)
CELLS = (
    [(2, j) for j in range(4)] + [(0, 2), (1, 2), (3, 2)]
    + [(1, 0), (1, 1), (1, 3), (0, 1), (3, 1)]
    + [(3, 0), (3, 3), (0, 3)]
    + [(0, 0)]
)
BLOCK = 64
EVEN = [(i, j) for j in (0, 2, 4) for i in range(j + 1)]
ODD = [(i, j) for j in (1, 3) for i in range(j + 1)]
PACK = [(i, j, n, 0) for n, (i, j) in enumerate(EVEN[:8])]
PACK += [(i, j, n, 1) for n, (i, j) in enumerate(ODD + EVEN[8:])]
TILES = 64
PIECE = TILES // 32
PART = HALF // SIDE


def table(q, values):
    return sum(jnp.where(q == k, v, 0) for k, v in enumerate(values) if v)


def reduce_kernel(
    slab, map_rows,
    sketch_t, m, cross_out,
    slab_v, map_t, parts, gpack, gsib, gred, gline, gtot,
    cross, from_core, from_a, from_b, line, from_y,
    load_sem, map_sem, out_sem,
    g0s, g0r, g1s, g1r, g2s, g2r, g3s, g3r,
    xs, xr, as_, ar, bs, br, ys, yr, zs, zr,
):
    g = lax.axis_index("grp")
    d = lax.axis_index("dev")
    y, c = g // 2, g % 2
    z, x = d // SIDE, d % SIDE
    other = g + 1 - 2 * c
    row_c = pl.multiple_of(c * HALF, 8)
    row_o = pl.multiple_of((1 - c) * HALF, 8)
    mine = pl.ds(row_c, HALF)

    map_copy = pltpu.make_async_copy(map_rows, map_t, map_sem)
    map_copy.start()

    def load(i):
        rows = pl.ds(pl.multiple_of(i * CHUNK, CHUNK), CHUNK)
        return pltpu.make_async_copy(slab.at[rows, :], slab_v.at[rows, :], load_sem.at[i])

    load(0).start()
    load(1).start()

    def chip(dz, dx):
        return lax.rem(z + dz, SIDE) * SIDE + lax.rem(x + dx, SIDE)

    def along_a(i):
        return jnp.where(c == 0, chip(i, 0), chip(0, i))

    def along_b(i):
        return jnp.where(c == 0, chip(0, i), chip(i, 0))

    def along_y(i, core):
        return lax.rem(y + i, SIDE) * 2 + core

    barrier = pltpu.get_barrier_semaphore()

    def greet(to_g, to_d):
        pl.semaphore_signal(barrier, inc=1, device_id=(to_g, to_d), device_id_type=MESH)

    for dz, dx in AROUND:
        greet(g, chip(dz, dx))
        greet(other, chip(dz, dx))
    for i in range(1, SIDE):
        greet(along_y(i, c), d)
    for i in range(SIDE):
        greet(along_y(i, 1 - c), d)

    map_copy.wait()

    def sketch_chunk(i, carry):
        load(i).wait()

        @pl.when(i + 2 < LOCAL // CHUNK)
        def _():
            load(i + 2).start()

        rows = pl.ds(pl.multiple_of(i * CHUNK, CHUNK), CHUNK)
        s = dot(map_t[...], slab_v[rows, :], NT)
        high, low = split(s)
        parts[:SK, rows] = high
        parts[SK:, rows] = low
        return carry

    lax.fori_loop(0, LOCAL // CHUNK, sketch_chunk, 0)
    sketch_out = pltpu.make_async_copy(parts, sketch_t, out_sem)
    sketch_out.start()

    mixed = dot(parts[SK:], parts[:SK], NT)
    gram = dot(parts[:SK], parts[:SK], NT) + (mixed + mixed.T)
    gpack[56:64] = jnp.zeros((8, 8, 128), F32)
    for i, j, n, h in PACK:
        block = gram[i * BLOCK : (i + 1) * BLOCK, j * BLOCK : (j + 1) * BLOCK]
        gpack[8 * n : 8 * n + 8, :, h * BLOCK : (h + 1) * BLOCK] = block.reshape(8, 8, BLOCK)

    pl.semaphore_wait(barrier, 2 * len(AROUND) + 2 * SIDE - 1)

    def remote(src, dst, send, recv, to_g, to_d):
        return pltpu.make_async_remote_copy(
            src_ref=src, dst_ref=dst, send_sem=send, recv_sem=recv,
            device_id=(to_g, to_d), device_id_type=MESH,
        )

    def core_copy(q):
        dz, dx = table(q, [p[0] for p in CELLS]), table(q, [p[1] for p in CELLS])
        here = jnp.where(c == 0, dz * SIDE + dx, dx * SIDE + dz)
        there = jnp.where(c == 0, dx * SIDE + dz, dz * SIDE + dx)
        return remote(
            cross.at[here, pl.ds(row_o, HALF), :], from_core.at[there],
            xs.at[q], xr.at[q], other, d,
        )

    def cross_cell(q):
        dz, dx = table(q, [p[0] for p in CELLS]), table(q, [p[1] for p in CELLS])
        here = jnp.where(c == 0, dz * SIDE + dx, dx * SIDE + dz)
        columns = pl.ds(pl.multiple_of(chip(dz, dx) * WIDTH, WIDTH), WIDTH)
        return here, dot(parts[:SK], slab_v[:, columns], NN)

    def cross_pair(t, carry):
        first, a = cross_cell(2 * t)
        second, b = cross_cell(2 * t + 1)
        cross[first] = a
        cross[second] = b
        core_copy(2 * t).start()
        core_copy(2 * t + 1).start()
        return carry

    def run_cross(first, last):
        lax.fori_loop(first // 2, last // 2, cross_pair, 0)

    def cross_arrived(first, last):
        def body(q, carry):
            core_copy(q).wait()
            return carry
        lax.fori_loop(first, last, body, 0)

    def add_core(p):
        cross[p, mine, :] += from_core[p]

    g0 = remote(gpack, gsib, g0s, g0r, other, d)
    g0.start()
    run_cross(0, 4)
    g0.wait()
    gsib[...] = gpack[...] + gsib[...]

    def g1(dz, dx):
        to = chip(dz, dx)
        k = dz * SIDE + dx
        part = pl.ds(c * (TILES // 2) + to * PIECE, PIECE)
        return remote(gsib.at[part], gred.at[k], g1s.at[k], g1r.at[k], g, to)

    for p in AROUND:
        g1(*p).start()
    run_cross(4, 8)

    def a_copy(k):
        first = (8, 10, 6, 12, 4, 14)[k]
        to = along_a(1 if k % 2 == 0 else SIDE - 1)
        return remote(
            cross.at[pl.ds(first, 2), mine, :], from_a.at[k], as_.at[k], ar.at[k], g, to
        )

    cross_arrived(0, 7)
    for p in range(8, 12):
        add_core(p)
    a_copy(0).start()
    a_copy(1).start()
    run_cross(8, 12)
    cross_arrived(7, 12)
    for p in range(4, 8):
        add_core(p)
    a_copy(2).start()
    run_cross(12, 16)

    for p in AROUND[::-1]:
        g1(*p).wait()
    part = pl.ds(c * (TILES // 2) + d * PIECE, PIECE)
    total = gsib[part]
    for dz, dx in AROUND:
        total = total + gred[dz * SIDE + dx]
    gline[pl.ds(y, 1)] = total[None]

    def g2(i):
        return remote(gline.at[y], gline.at[y], g2s.at[i], g2r.at[i], along_y(i, c), d)

    for i in (2, 1, 3):
        g2(i).start()

    cross_arrived(12, 16)
    for p in range(12, 16):
        add_core(p)
    a_copy(3).start()
    for p in range(4):
        add_core(p)

    for i in (1, 3, 2):
        g2(i).wait()
    gtot[part] = (gline[0] + gline[1]) + (gline[2] + gline[3])

    def g3(flip, dz, dx):
        k = flip * SLICES + dz * SIDE + dx
        to_g = other if flip else g
        return remote(gtot.at[part], gtot.at[part], g3s.at[k], g3r.at[k], to_g, chip(dz, dx))

    handed = [(flip, dz, dx) for dz, dx in AROUND for flip in (0, 1)] + [(1, 0, 0)]
    for p in handed:
        g3(*p).start()

    a_copy(0).wait()
    a_copy(1).wait()
    cross[4:6, mine, :] += from_a[0]
    cross[14:16, mine, :] += from_a[1]
    a_copy(4).start()
    a_copy(5).start()
    m[...] = jnp.zeros_like(m)

    for k in range(2, 6):
        a_copy(k).wait()
    cross[0:2, mine, :] += from_a[4] + from_a[3]
    cross[2:4, mine, :] += from_a[2] + from_a[5]

    def b_copy(i):
        return remote(cross.at[i, mine, :], from_b.at[i], bs.at[i], br.at[i], g, along_b(i))

    for i in (2, 1, 3):
        b_copy(i).start()

    for p in handed[::-1]:
        g3(*p).wait()
    for i, j, n, h in PACK:
        block = gtot[8 * n : 8 * n + 8, :, h * BLOCK : (h + 1) * BLOCK].reshape(BLOCK, BLOCK)
        m[i * BLOCK : (i + 1) * BLOCK, j * BLOCK : (j + 1) * BLOCK] = block

    def factor_step(k):
        invert_step(m, k, SK, BLOCK, 16)

    factor_step(0)
    for i in (1, 3, 2):
        b_copy(i).wait()
    line[...] = (cross[0, mine, :] + from_b[1]) + (from_b[2] + from_b[3])

    def y_copy(i):
        rows = pl.ds(pl.multiple_of(lax.rem(y + i, SIDE) * PART, 8), PART)
        return remote(line.at[rows, :], from_y.at[i], ys.at[i], yr.at[i], along_y(i, c), d)

    for i in (2, 1, 3):
        y_copy(i).start()
    factor_step(1)
    factor_step(2)
    for i in (1, 3, 2):
        y_copy(i).wait()
    own = line[pl.ds(pl.multiple_of(y * PART, 8), PART), :]
    final = pl.ds(pl.multiple_of(c * HALF + y * PART, 8), PART)
    cross_out[final, :] = (own + from_y[1]) + (from_y[2] + from_y[3])

    def z_copy(k):
        i, flip = k % SIDE, k // SIDE
        core = c + flip * (1 - 2 * c)
        return remote(
            cross_out.at[final, :], cross_out.at[final, :], zs.at[k], zr.at[k],
            along_y(i, core), d,
        )

    for k in range(1, 2 * SIDE):
        z_copy(k).start()
    factor_step(3)
    factor_step(4)
    for k in range(1, 2 * SIDE):
        z_copy(k).wait()
    sketch_out.wait()


def reduce_call(slab, map_rows):
    dma = pltpu.SemaphoreType.DMA
    return pl.pallas_call(
        reduce_kernel,
        out_shape=(
            jax.ShapeDtypeStruct((2 * SK, LOCAL), BF16),
            jax.ShapeDtypeStruct((SK, SK), F32),
            jax.ShapeDtypeStruct((SK, WIDTH), F32),
        ),
        in_specs=[pl.BlockSpec(memory_space=pl.ANY)] * 2,
        out_specs=(
            pl.BlockSpec(memory_space=pl.ANY),
            pl.BlockSpec(memory_space=pltpu.VMEM),
            pl.BlockSpec(memory_space=pltpu.VMEM),
        ),
        scratch_shapes=[
            pltpu.VMEM((LOCAL, N), BF16),
            pltpu.VMEM((SK, N), BF16),
            pltpu.VMEM((2 * SK, LOCAL), BF16),
            pltpu.VMEM((TILES, 8, 128), F32),
            pltpu.VMEM((TILES, 8, 128), F32),
            pltpu.VMEM((SLICES, PIECE, 8, 128), F32),
            pltpu.VMEM((SIDE, PIECE, 8, 128), F32),
            pltpu.VMEM((TILES, 8, 128), F32),
            pltpu.VMEM((SLICES, SK, WIDTH), F32),
            pltpu.VMEM((SLICES, HALF, WIDTH), F32),
            pltpu.VMEM((6, 2, HALF, WIDTH), F32),
            pltpu.VMEM((SIDE, HALF, WIDTH), F32),
            pltpu.VMEM((HALF, WIDTH), F32),
            pltpu.VMEM((SIDE, PART, WIDTH), F32),
            dma((LOCAL // CHUNK,)), dma, dma,
            dma, dma,
            dma((SLICES,)), dma((SLICES,)),
            dma((SIDE,)), dma((SIDE,)),
            dma((2 * SLICES,)), dma((2 * SLICES,)),
            dma((SLICES,)), dma((SLICES,)),
            dma((6,)), dma((6,)),
            dma((SIDE,)), dma((SIDE,)),
            dma((SIDE,)), dma((SIDE,)),
            dma((2 * SIDE,)), dma((2 * SIDE,)),
        ],
        compiler_params=pltpu.CompilerParams(
            collective_id=0, has_side_effects=True, vmem_limit_bytes=58 << 20
        ),
        cost_estimate=pl.CostEstimate(
            flops=4 * LOCAL * N * SK, bytes_accessed=24 << 20, transcendentals=0
        ),
        name="sketch_and_sums",
    )(slab, map_rows)


def finish_kernel(
    scale, inverse, cross, sketch_t, basis_t, coeffs, m, cr, lefts, parts, out, m_sem, cross_sem, load_sem, out_sem
):
    m_copy = pltpu.make_async_copy(inverse, m, m_sem)
    m_copy.start()

    def load(i):
        part = pl.ds(pl.multiple_of(i * STEP, STEP), STEP)
        return pltpu.make_async_copy(sketch_t.at[:, part], parts.at[:, part], load_sem.at[i])

    for i in range(LOCAL // STEP):
        load(i).start()
    cross_copy = pltpu.make_async_copy(cross, cr, cross_sem)
    cross_copy.start()
    m_copy.wait()
    high, low = split(m[...] * scale)
    lefts[...] = jnp.concatenate([high, high, low], axis=1)

    def store(i):
        part = pl.ds(pl.multiple_of(i * STEP, STEP), STEP)
        return pltpu.make_async_copy(out.at[:, part], basis_t.at[:, part], out_sem.at[i])

    def basis_chunk(i, carry):
        part = pl.ds(pl.multiple_of(i * STEP, STEP), STEP)
        load(i).wait()
        right = jnp.concatenate([parts[:, part], parts[:SK, part]], axis=0)
        out[:, part] = dot(lefts[...], right, NN)
        store(i).start()
        return carry

    lax.fori_loop(0, LOCAL // STEP, basis_chunk, 0)
    cross_copy.wait()
    coeffs[...] = dot3(m[...], cr[...], NN) * (1.0 / scale)
    for i in range(LOCAL // STEP):
        store(i).wait()


def finish_call(scale, inverse, cross, sketch_t):
    def kernel(*refs):
        finish_kernel(scale, *refs)

    vmem = pl.BlockSpec(memory_space=pltpu.VMEM)
    hbm = pl.BlockSpec(memory_space=pl.ANY)
    dma = pltpu.SemaphoreType.DMA
    return pl.pallas_call(
        kernel,
        out_shape=(
            jax.ShapeDtypeStruct((SK, LOCAL), F32),
            jax.ShapeDtypeStruct((SK, WIDTH), F32),
        ),
        in_specs=[hbm, hbm, hbm],
        out_specs=(hbm, vmem),
        scratch_shapes=[
            pltpu.VMEM((SK, SK), F32),
            pltpu.VMEM((SK, WIDTH), F32),
            pltpu.VMEM((SK, 3 * SK), BF16),
            pltpu.VMEM((2 * SK, LOCAL), BF16),
            pltpu.VMEM((SK, LOCAL), F32),
            dma, dma,
            dma((LOCAL // STEP,)), dma((LOCAL // STEP,)),
        ],
        compiler_params=pltpu.CompilerParams(vmem_limit_bytes=60 << 20),
        name="basis_and_coeffs",
    )(inverse, cross, sketch_t)


def local(slab, sketch_map):
    rows = slab.shape[0] * lax.axis_size("grp") * lax.axis_size("dev")
    scale = math.sqrt(rows)
    sketch_t, inverse, cross = reduce_call(slab, sketch_map.T)
    basis_t, coeffs = finish_call(scale, inverse, cross, sketch_t)
    return basis_t.T, coeffs


def solution(mesh):
    in_specs = (P(("grp", "dev"), None), P())
    out_specs = (P(("grp", "dev"), None), P(None, "dev"))
    return jax.shard_map(local, mesh=mesh, in_specs=in_specs, out_specs=out_specs, check_vma=False)
```

```python
import math

import jax
import jax.numpy as jnp
from jax import lax
from jax.experimental import pallas as pl
from jax.experimental.pallas import tpu as pltpu
from jax.sharding import PartitionSpec as P

F32 = jnp.float32
BF16 = jnp.bfloat16
NN = (((1,), (0,)), ((), ()))
NT = (((1,), (1,)), ((), ()))
TN = (((0,), (0,)), ((), ()))
MESH = pl.DeviceIdType.MESH

N = 4096
SK = 320
HALF = SK // 2
LOCAL = 2048
CHUNK = 512
STEP = 1024
WIDTH = 256
SLICES = 16
SIDE = 4


def dot(a, b, dims):
    return lax.dot_general(a, b, dims, preferred_element_type=F32)


def split(a):
    high = a.astype(BF16)
    return high, (a - high.astype(F32)).astype(BF16)


def dot3(a, b, dims):
    ah, al = split(a)
    bh, bl = split(b)
    return dot(ah, bh, dims) + (dot(ah, bl, dims) + dot(al, bh, dims))


def factor_block(a, n, w):
    eye = lax.broadcasted_iota(jnp.int32, (n, n), 0) == lax.broadcasted_iota(jnp.int32, (n, n), 1)
    m = jnp.concatenate([a, eye.astype(F32)], axis=1)
    width = 2 * n
    row_in_group = lax.broadcasted_iota(jnp.int32, (8, width), 0)
    per = w // 8
    groups = [m[8 * g : 8 * g + 8] for g in range(n // 8)]
    done = []

    def spread(value, i):
        return jnp.broadcast_to(value[i : i + 1], (8, width))

    for p in range(n // w):
        rows = groups[p * per :]
        cols = [
            [jnp.broadcast_to(r[:, p * w + l : p * w + l + 1], (8, width)) for r in rows]
            for l in range(w)
        ]
        pivots = [jnp.ones((8, width), F32) for _ in range(per)]
        for k in range(w):
            g, i = divmod(k, 8)
            pivot = spread(cols[k][g], i)
            inverse = 1.0 / pivot
            left = range(g, len(rows))
            factor = {h: cols[k][h] * inverse for h in left}
            factor[g] = jnp.where(row_in_group > i, factor[g], 0.0)
            for l in range(k + 1, w):
                value = spread(cols[l][g], i)
                for h in left:
                    cols[l][h] = cols[l][h] - factor[h] * value
            value = spread(rows[g], i)
            for h in left:
                rows[h] = rows[h] - factor[h] * value
            pivots[g] = jnp.where(row_in_group == i, pivot, pivots[g])
        for h in range(per):
            done.append((rows[h] * lax.rsqrt(pivots[h]))[:, n:])
        groups[p * per :] = rows
    return jnp.concatenate(done, axis=0)


def invert_step(m, k, n, b, w):
    lo, hi = k * b, (k + 1) * b
    t = factor_block(m[lo:hi, lo:hi], b, w)
    r = dot3(t, m[lo:hi, :], NN)
    parts = [r[:, :lo]] if lo else []
    parts.append(t)
    if hi < n:
        parts.append(r[:, hi:])
    r = jnp.concatenate(parts, axis=1)
    if hi < n:
        col = lax.broadcasted_iota(jnp.int32, (n - hi, n), 1)
        keep = jnp.where((col >= lo) & (col < hi), 0.0, m[hi:, :])
        m[hi:, :] = keep - dot3(r[:, hi:], r, TN)
        col = lax.broadcasted_iota(jnp.int32, (b, n), 1)
        r = jnp.where(col < hi, r, 0.0)
    m[lo:hi, :] = r


DIST = (0, 1, 2, 1)
AROUND = sorted(
    ((i, j) for i in range(SIDE) for j in range(SIDE) if (i, j) != (0, 0)),
    key=lambda p: -(DIST[p[0]] + DIST[p[1]]),
)
CELLS = (
    [(2, j) for j in range(4)] + [(0, 2), (1, 2), (3, 2)]
    + [(1, 0), (1, 1), (1, 3), (0, 1), (3, 1)]
    + [(3, 0), (3, 3), (0, 3)]
    + [(0, 0)]
)
BLOCK = 64
EVEN = [(i, j) for j in (0, 2, 4) for i in range(j + 1)]
ODD = [(i, j) for j in (1, 3) for i in range(j + 1)]
PACK = [(i, j, n, 0) for n, (i, j) in enumerate(EVEN[:8])]
PACK += [(i, j, n, 1) for n, (i, j) in enumerate(ODD + EVEN[8:])]
TILES = 64
PIECE = TILES // 32
PART = HALF // SIDE


def wait_store(store):
    def body(i, carry):
        store(i).wait()
        return carry

    return body


def table(q, values):
    return sum(jnp.where(q == k, v, 0) for k, v in enumerate(values) if v)


def whole_kernel(
    scale, slab, map_rows,
    basis_t, coeffs,
    m, cross_out, left, out, slab_v, map_t, parts, gpack, gsib, gred, gline, gtot,
    cross, from_core, from_a, from_b, line, from_y,
    load_sem, map_sem, out_sem,
    g0s, g0r, g1s, g1r, g2s, g2r, g3s, g3r,
    xs, xr, as_, ar, bs, br, ys, yr, zs, zr,
):
    g = lax.axis_index("grp")
    d = lax.axis_index("dev")
    y, c = g // 2, g % 2
    z, x = d // SIDE, d % SIDE
    other = g + 1 - 2 * c
    row_c = pl.multiple_of(c * HALF, 8)
    row_o = pl.multiple_of((1 - c) * HALF, 8)
    mine = pl.ds(row_c, HALF)

    map_copy = pltpu.make_async_copy(map_rows, map_t, map_sem)
    map_copy.start()

    def load(i):
        rows = pl.ds(pl.multiple_of(i * CHUNK, CHUNK), CHUNK)
        return pltpu.make_async_copy(slab.at[rows, :], slab_v.at[rows, :], load_sem.at[i])

    load(0).start()
    load(1).start()

    def chip(dz, dx):
        return lax.rem(z + dz, SIDE) * SIDE + lax.rem(x + dx, SIDE)

    def along_a(i):
        return jnp.where(c == 0, chip(i, 0), chip(0, i))

    def along_b(i):
        return jnp.where(c == 0, chip(0, i), chip(i, 0))

    def along_y(i, core):
        return lax.rem(y + i, SIDE) * 2 + core

    barrier = pltpu.get_barrier_semaphore()

    def greet(to_g, to_d):
        pl.semaphore_signal(barrier, inc=1, device_id=(to_g, to_d), device_id_type=MESH)

    for dz, dx in AROUND:
        greet(g, chip(dz, dx))
        greet(other, chip(dz, dx))
    for i in range(1, SIDE):
        greet(along_y(i, c), d)
    for i in range(SIDE):
        greet(along_y(i, 1 - c), d)

    map_copy.wait()

    def sketch_chunk(i, carry):
        load(i).wait()

        @pl.when(i + 2 < LOCAL // CHUNK)
        def _():
            load(i + 2).start()

        rows = pl.ds(pl.multiple_of(i * CHUNK, CHUNK), CHUNK)
        s = dot(map_t[...], slab_v[rows, :], NT)
        high, low = split(s)
        parts[:SK, rows] = high
        parts[SK:, rows] = low
        return carry

    lax.fori_loop(0, LOCAL // CHUNK, sketch_chunk, 0)

    mixed = dot(parts[SK:], parts[:SK], NT)
    gram = dot(parts[:SK], parts[:SK], NT) + (mixed + mixed.T)
    gpack[56:64] = jnp.zeros((8, 8, 128), F32)
    for i, j, n, h in PACK:
        block = gram[i * BLOCK : (i + 1) * BLOCK, j * BLOCK : (j + 1) * BLOCK]
        gpack[8 * n : 8 * n + 8, :, h * BLOCK : (h + 1) * BLOCK] = block.reshape(8, 8, BLOCK)

    pl.semaphore_wait(barrier, 2 * len(AROUND) + 2 * SIDE - 1)

    def remote(src, dst, send, recv, to_g, to_d):
        return pltpu.make_async_remote_copy(
            src_ref=src, dst_ref=dst, send_sem=send, recv_sem=recv,
            device_id=(to_g, to_d), device_id_type=MESH,
        )

    def core_copy(q):
        dz, dx = table(q, [p[0] for p in CELLS]), table(q, [p[1] for p in CELLS])
        here = jnp.where(c == 0, dz * SIDE + dx, dx * SIDE + dz)
        there = jnp.where(c == 0, dx * SIDE + dz, dz * SIDE + dx)
        return remote(
            cross.at[here, pl.ds(row_o, HALF), :], from_core.at[there],
            xs.at[q], xr.at[q], other, d,
        )

    def cross_cell(q):
        dz, dx = table(q, [p[0] for p in CELLS]), table(q, [p[1] for p in CELLS])
        here = jnp.where(c == 0, dz * SIDE + dx, dx * SIDE + dz)
        columns = pl.ds(pl.multiple_of(chip(dz, dx) * WIDTH, WIDTH), WIDTH)
        return here, dot(parts[:SK], slab_v[:, columns], NN)

    def cross_pair(t, carry):
        first, a = cross_cell(2 * t)
        second, b = cross_cell(2 * t + 1)
        cross[first] = a
        cross[second] = b
        core_copy(2 * t).start()
        core_copy(2 * t + 1).start()
        return carry

    def run_cross(first, last):
        lax.fori_loop(first // 2, last // 2, cross_pair, 0)

    def cross_arrived(first, last):
        def body(q, carry):
            core_copy(q).wait()
            return carry
        lax.fori_loop(first, last, body, 0)

    def add_core(p):
        cross[p, mine, :] += from_core[p]

    g0 = remote(gpack, gsib, g0s, g0r, other, d)
    g0.start()
    run_cross(0, 4)
    g0.wait()
    gsib[...] = gpack[...] + gsib[...]

    def g1(dz, dx):
        to = chip(dz, dx)
        k = dz * SIDE + dx
        part = pl.ds(c * (TILES // 2) + to * PIECE, PIECE)
        return remote(gsib.at[part], gred.at[k], g1s.at[k], g1r.at[k], g, to)

    for p in AROUND:
        g1(*p).start()
    run_cross(4, 8)

    def a_copy(k):
        first = (8, 10, 6, 12, 4, 14)[k]
        to = along_a(1 if k % 2 == 0 else SIDE - 1)
        return remote(
            cross.at[pl.ds(first, 2), mine, :], from_a.at[k], as_.at[k], ar.at[k], g, to
        )

    cross_arrived(0, 7)
    for p in range(8, 12):
        add_core(p)
    a_copy(0).start()
    a_copy(1).start()
    run_cross(8, 12)
    cross_arrived(7, 12)
    for p in range(4, 8):
        add_core(p)
    a_copy(2).start()
    run_cross(12, 16)

    for p in AROUND[::-1]:
        g1(*p).wait()
    part = pl.ds(c * (TILES // 2) + d * PIECE, PIECE)
    total = gsib[part]
    for dz, dx in AROUND:
        total = total + gred[dz * SIDE + dx]
    gline[pl.ds(y, 1)] = total[None]

    def g2(i):
        return remote(gline.at[y], gline.at[y], g2s.at[i], g2r.at[i], along_y(i, c), d)

    for i in (2, 1, 3):
        g2(i).start()

    cross_arrived(12, 16)
    for p in range(12, 16):
        add_core(p)
    a_copy(3).start()
    for p in range(4):
        add_core(p)

    for i in (1, 3, 2):
        g2(i).wait()
    gtot[part] = (gline[0] + gline[1]) + (gline[2] + gline[3])

    def g3(flip, dz, dx):
        k = flip * SLICES + dz * SIDE + dx
        to_g = other if flip else g
        return remote(gtot.at[part], gtot.at[part], g3s.at[k], g3r.at[k], to_g, chip(dz, dx))

    handed = [(flip, dz, dx) for dz, dx in AROUND for flip in (0, 1)] + [(1, 0, 0)]
    for p in handed:
        g3(*p).start()

    a_copy(0).wait()
    a_copy(1).wait()
    cross[4:6, mine, :] += from_a[0]
    cross[14:16, mine, :] += from_a[1]
    a_copy(4).start()
    a_copy(5).start()
    m[...] = jnp.zeros_like(m)

    for k in range(2, 6):
        a_copy(k).wait()
    cross[0:2, mine, :] += from_a[4] + from_a[3]
    cross[2:4, mine, :] += from_a[2] + from_a[5]

    def b_copy(i):
        return remote(cross.at[i, mine, :], from_b.at[i], bs.at[i], br.at[i], g, along_b(i))

    for i in (2, 1, 3):
        b_copy(i).start()

    for p in handed[::-1]:
        g3(*p).wait()
    for i, j, n, h in PACK:
        block = gtot[8 * n : 8 * n + 8, :, h * BLOCK : (h + 1) * BLOCK].reshape(BLOCK, BLOCK)
        m[i * BLOCK : (i + 1) * BLOCK, j * BLOCK : (j + 1) * BLOCK] = block

    def factor_step(k):
        invert_step(m, k, SK, BLOCK, 16)

    factor_step(0)
    for i in (1, 3, 2):
        b_copy(i).wait()
    line[...] = (cross[0, mine, :] + from_b[1]) + (from_b[2] + from_b[3])

    def y_copy(i):
        rows = pl.ds(pl.multiple_of(lax.rem(y + i, SIDE) * PART, 8), PART)
        return remote(line.at[rows, :], from_y.at[i], ys.at[i], yr.at[i], along_y(i, c), d)

    for i in (2, 1, 3):
        y_copy(i).start()
    factor_step(1)
    factor_step(2)
    for i in (1, 3, 2):
        y_copy(i).wait()
    own = line[pl.ds(pl.multiple_of(y * PART, 8), PART), :]
    final = pl.ds(pl.multiple_of(c * HALF + y * PART, 8), PART)
    cross_out[final, :] = (own + from_y[1]) + (from_y[2] + from_y[3])

    def z_copy(k):
        i, flip = k % SIDE, k // SIDE
        core = c + flip * (1 - 2 * c)
        return remote(
            cross_out.at[final, :], cross_out.at[final, :], zs.at[k], zr.at[k],
            along_y(i, core), d,
        )

    for k in range(1, 2 * SIDE):
        z_copy(k).start()
    factor_step(3)
    factor_step(4)

    high, low = split(m[...] * scale)
    left[...] = jnp.concatenate([high, high, low], axis=1)

    def store(i):
        part = pl.ds(pl.multiple_of(i * STEP, STEP), STEP)
        return pltpu.make_async_copy(out.at[:, part], basis_t.at[:, part], out_sem.at[i])

    def basis_step(i, carry):
        part = pl.ds(pl.multiple_of(i * STEP, STEP), STEP)
        right = jnp.concatenate([parts[:, part], parts[:SK, part]], axis=0)
        out[:, part] = dot(left[...], right, NN)
        store(i).start()
        return carry

    lax.fori_loop(0, LOCAL // STEP, basis_step, 0)
    for k in range(1, 2 * SIDE):
        z_copy(k).wait()
    coeffs[...] = dot3(m[...], cross_out[...], NN) * (1.0 / scale)
    lax.fori_loop(0, LOCAL // STEP, wait_store(store), 0)


def whole_call(scale, slab, map_rows):
    def kernel(*refs):
        whole_kernel(scale, *refs)

    dma = pltpu.SemaphoreType.DMA
    return pl.pallas_call(
        kernel,
        out_shape=(
            jax.ShapeDtypeStruct((SK, LOCAL), F32),
            jax.ShapeDtypeStruct((SK, WIDTH), F32),
        ),
        in_specs=[pl.BlockSpec(memory_space=pl.ANY)] * 2,
        out_specs=(
            pl.BlockSpec(memory_space=pl.ANY),
            pl.BlockSpec(memory_space=pltpu.VMEM),
        ),
        scratch_shapes=[
            pltpu.VMEM((SK, SK), F32),
            pltpu.VMEM((SK, WIDTH), F32),
            pltpu.VMEM((SK, 3 * SK), BF16),
            pltpu.VMEM((SK, LOCAL), F32),
            pltpu.VMEM((LOCAL, N), BF16),
            pltpu.VMEM((SK, N), BF16),
            pltpu.VMEM((2 * SK, LOCAL), BF16),
            pltpu.VMEM((TILES, 8, 128), F32),
            pltpu.VMEM((TILES, 8, 128), F32),
            pltpu.VMEM((SLICES, PIECE, 8, 128), F32),
            pltpu.VMEM((SIDE, PIECE, 8, 128), F32),
            pltpu.VMEM((TILES, 8, 128), F32),
            pltpu.VMEM((SLICES, SK, WIDTH), F32),
            pltpu.VMEM((SLICES, HALF, WIDTH), F32),
            pltpu.VMEM((6, 2, HALF, WIDTH), F32),
            pltpu.VMEM((SIDE, HALF, WIDTH), F32),
            pltpu.VMEM((HALF, WIDTH), F32),
            pltpu.VMEM((SIDE, PART, WIDTH), F32),
            dma((LOCAL // CHUNK,)), dma, dma((LOCAL // STEP,)),
            dma, dma,
            dma((SLICES,)), dma((SLICES,)),
            dma((SIDE,)), dma((SIDE,)),
            dma((2 * SLICES,)), dma((2 * SLICES,)),
            dma((SLICES,)), dma((SLICES,)),
            dma((6,)), dma((6,)),
            dma((SIDE,)), dma((SIDE,)),
            dma((SIDE,)), dma((SIDE,)),
            dma((2 * SIDE,)), dma((2 * SIDE,)),
        ],
        compiler_params=pltpu.CompilerParams(
            collective_id=0, has_side_effects=True, vmem_limit_bytes=58 << 20
        ),
        cost_estimate=pl.CostEstimate(
            flops=4 * LOCAL * N * SK, bytes_accessed=24 << 20, transcendentals=0
        ),
        name="range_finder",
    )(slab, map_rows)


def local(slab, sketch_map):
    rows = slab.shape[0] * lax.axis_size("grp") * lax.axis_size("dev")
    scale = math.sqrt(rows)
    basis_t, coeffs = whole_call(scale, slab, sketch_map.T)
    return basis_t.T, coeffs


def solution(mesh):
    in_specs = (P(("grp", "dev"), None), P())
    out_specs = (P(("grp", "dev"), None), P(None, "dev"))
    return jax.shard_map(local, mesh=mesh, in_specs=in_specs, out_specs=out_specs, check_vma=False)
```

```python
import math

import jax
import jax.numpy as jnp
from jax import lax
from jax.experimental import pallas as pl
from jax.experimental.pallas import tpu as pltpu
from jax.sharding import PartitionSpec as P

F32 = jnp.float32
BF16 = jnp.bfloat16
NN = (((1,), (0,)), ((), ()))
NT = (((1,), (1,)), ((), ()))
TN = (((0,), (0,)), ((), ()))
MESH = pl.DeviceIdType.MESH

N = 4096
SK = 320
HALF = SK // 2
LOCAL = 2048
CHUNK = 512
STEP = 1024
HAND = 8
WIDTH = 256
SLICES = 16
SIDE = 4


def dot(a, b, dims):
    return lax.dot_general(a, b, dims, preferred_element_type=F32)


def split(a):
    high = a.astype(BF16)
    return high, (a - high.astype(F32)).astype(BF16)


def dot3(a, b, dims):
    ah, al = split(a)
    bh, bl = split(b)
    (ca,), (cb,) = dims[0]
    return dot(jnp.concatenate([ah, al, ah], axis=ca), jnp.concatenate([bh, bh, bl], axis=cb), dims)


def factor_block(a, n, w):
    eye = lax.broadcasted_iota(jnp.int32, (n, n), 0) == lax.broadcasted_iota(jnp.int32, (n, n), 1)
    m = jnp.concatenate([a, eye.astype(F32)], axis=1)
    width = 2 * n
    row_in_group = lax.broadcasted_iota(jnp.int32, (8, width), 0)
    per = w // 8
    groups = [m[8 * g : 8 * g + 8] for g in range(n // 8)]
    done = []

    def spread(value, i):
        return jnp.broadcast_to(value[i : i + 1], (8, width))

    for p in range(n // w):
        rows = groups[p * per :]
        cols = [
            [jnp.broadcast_to(r[:, p * w + l : p * w + l + 1], (8, width)) for r in rows]
            for l in range(w)
        ]
        pivots = [jnp.ones((8, width), F32) for _ in range(per)]
        for k in range(w):
            g, i = divmod(k, 8)
            pivot = spread(cols[k][g], i)
            inverse = 1.0 / pivot
            left = range(g, len(rows))
            factor = {h: cols[k][h] * inverse for h in left}
            factor[g] = jnp.where(row_in_group > i, factor[g], 0.0)
            for l in range(k + 1, w):
                value = spread(cols[l][g], i)
                for h in left:
                    cols[l][h] = cols[l][h] - factor[h] * value
            value = spread(rows[g], i)
            for h in left:
                rows[h] = rows[h] - factor[h] * value
            pivots[g] = jnp.where(row_in_group == i, pivot, pivots[g])
        for h in range(per):
            done.append((rows[h] * lax.rsqrt(pivots[h]))[:, n:])
        groups[p * per :] = rows
    return jnp.concatenate(done, axis=0)


def invert_step(m, k, n, b, w):
    lo, hi = k * b, (k + 1) * b
    t = factor_block(m[lo:hi, lo:hi], b, w)
    r = dot3(t, m[lo:hi, :], NN)
    parts = [r[:, :lo]] if lo else []
    parts.append(t)
    if hi < n:
        parts.append(r[:, hi:])
    r = jnp.concatenate(parts, axis=1)
    if hi < n:
        col = lax.broadcasted_iota(jnp.int32, (n - hi, n), 1)
        keep = jnp.where((col >= lo) & (col < hi), 0.0, m[hi:, :])
        m[hi:, :] = keep - dot3(r[:, hi:], r, TN)
        col = lax.broadcasted_iota(jnp.int32, (b, n), 1)
        r = jnp.where(col < hi, r, 0.0)
    m[lo:hi, :] = r


DIST = (0, 1, 2, 1)
AROUND = sorted(
    ((i, j) for i in range(SIDE) for j in range(SIDE) if (i, j) != (0, 0)),
    key=lambda p: -(DIST[p[0]] + DIST[p[1]]),
)
CELLS = (
    [(2, j) for j in range(4)] + [(0, 2), (1, 2), (3, 2)]
    + [(1, 0), (1, 1), (1, 3), (0, 1), (3, 1)]
    + [(3, 0), (3, 3), (0, 3)]
    + [(0, 0)]
)
BLOCK = 64
EVEN = [(i, j) for j in (0, 2, 4) for i in range(j + 1)]
ODD = [(i, j) for j in (1, 3) for i in range(j + 1)]
PACK = [(i, j, n, 0) for n, (i, j) in enumerate(EVEN[:8])]
PACK += [(i, j, n, 1) for n, (i, j) in enumerate(ODD + EVEN[8:])]
TILES = 64
PIECE = TILES // 32
PART = HALF // SIDE


def wait_store(store):
    def body(i, carry):
        store(i).wait()
        return carry

    return body


def table(q, values):
    return sum(jnp.where(q == k, v, 0) for k, v in enumerate(values) if v)


def whole_kernel(
    scale, slab, map_rows,
    basis_t, coeffs,
    m, cross_out, left, out, slab_v, map_t, parts, gpack, gsib, gred, gline, gtot,
    cross, from_core, from_a, from_b, line, from_y,
    load_sem, map_sem, out_sem,
    g0s, g0r, g1s, g1r, g2s, g2r, g3s, g3r,
    xs, xr, as_, ar, bs, br, ys, yr, zs, zr,
):
    g = lax.axis_index("grp")
    d = lax.axis_index("dev")
    y, c = g // 2, g % 2
    z, x = d // SIDE, d % SIDE
    other = g + 1 - 2 * c
    row_c = pl.multiple_of(c * HALF, 8)
    row_o = pl.multiple_of((1 - c) * HALF, 8)
    mine = pl.ds(row_c, HALF)

    map_copy = pltpu.make_async_copy(map_rows, map_t, map_sem)
    map_copy.start()

    def load(i):
        rows = pl.ds(pl.multiple_of(i * CHUNK, CHUNK), CHUNK)
        return pltpu.make_async_copy(slab.at[rows, :], slab_v.at[rows, :], load_sem.at[i])

    load(0).start()
    load(1).start()

    def chip(dz, dx):
        return lax.rem(z + dz, SIDE) * SIDE + lax.rem(x + dx, SIDE)

    def along_a(i):
        return jnp.where(c == 0, chip(i, 0), chip(0, i))

    def along_b(i):
        return jnp.where(c == 0, chip(0, i), chip(i, 0))

    def along_y(i, core):
        return lax.rem(y + i, SIDE) * 2 + core

    barrier = pltpu.get_barrier_semaphore()

    def greet(to_g, to_d):
        pl.semaphore_signal(barrier, inc=1, device_id=(to_g, to_d), device_id_type=MESH)

    for dz, dx in AROUND:
        greet(g, chip(dz, dx))
        greet(other, chip(dz, dx))
    for i in range(1, SIDE):
        greet(along_y(i, c), d)
    for i in range(SIDE):
        greet(along_y(i, 1 - c), d)

    map_copy.wait()

    def sketch_chunk(i, carry):
        load(i).wait()

        @pl.when(i + 2 < LOCAL // CHUNK)
        def _():
            load(i + 2).start()

        rows = pl.ds(pl.multiple_of(i * CHUNK, CHUNK), CHUNK)
        s = dot(map_t[...], slab_v[rows, :], NT)
        high, low = split(s)
        parts[:SK, rows] = high
        parts[SK:, rows] = low
        return carry

    lax.fori_loop(0, LOCAL // CHUNK, sketch_chunk, 0)

    mixed = dot(parts[SK:], parts[:SK], NT)
    gram = dot(parts[:SK], parts[:SK], NT) + (mixed + mixed.T)
    gpack[56:64] = jnp.zeros((8, 8, 128), F32)
    for i, j, n, h in PACK:
        block = gram[i * BLOCK : (i + 1) * BLOCK, j * BLOCK : (j + 1) * BLOCK]
        gpack[8 * n : 8 * n + 8, :, h * BLOCK : (h + 1) * BLOCK] = block.reshape(8, 8, BLOCK)

    pl.semaphore_wait(barrier, 2 * len(AROUND) + 2 * SIDE - 1)

    def remote(src, dst, send, recv, to_g, to_d):
        return pltpu.make_async_remote_copy(
            src_ref=src, dst_ref=dst, send_sem=send, recv_sem=recv,
            device_id=(to_g, to_d), device_id_type=MESH,
        )

    def core_copy(q):
        dz, dx = table(q, [p[0] for p in CELLS]), table(q, [p[1] for p in CELLS])
        here = jnp.where(c == 0, dz * SIDE + dx, dx * SIDE + dz)
        there = jnp.where(c == 0, dx * SIDE + dz, dz * SIDE + dx)
        return remote(
            cross.at[here, pl.ds(row_o, HALF), :], from_core.at[there],
            xs.at[q], xr.at[q], other, d,
        )

    def cross_cell(q):
        dz, dx = table(q, [p[0] for p in CELLS]), table(q, [p[1] for p in CELLS])
        here = jnp.where(c == 0, dz * SIDE + dx, dx * SIDE + dz)
        columns = pl.ds(pl.multiple_of(chip(dz, dx) * WIDTH, WIDTH), WIDTH)
        return here, dot(parts[:SK], slab_v[:, columns], NN)

    def cross_pair(t, carry):
        first, a = cross_cell(2 * t)
        second, b = cross_cell(2 * t + 1)
        cross[first] = a
        cross[second] = b
        core_copy(2 * t).start()
        core_copy(2 * t + 1).start()
        return carry

    def run_cross(first, last):
        lax.fori_loop(first // 2, last // 2, cross_pair, 0)

    def cross_arrived(first, last):
        def body(q, carry):
            core_copy(q).wait()
            return carry
        lax.fori_loop(first, last, body, 0)

    def add_core(p):
        cross[p, mine, :] += from_core[p]

    g0 = remote(gpack, gsib, g0s, g0r, other, d)
    g0.start()
    run_cross(0, 4)
    g0.wait()
    gsib[...] = gpack[...] + gsib[...]

    def g1(dz, dx):
        to = chip(dz, dx)
        k = dz * SIDE + dx
        part = pl.ds(c * (TILES // 2) + to * PIECE, PIECE)
        return remote(gsib.at[part], gred.at[k], g1s.at[k], g1r.at[k], g, to)

    for p in AROUND:
        g1(*p).start()
    run_cross(4, 8)

    def a_copy(k):
        first = (8, 10, 6, 12, 4, 14)[k]
        to = along_a(1 if k % 2 == 0 else SIDE - 1)
        return remote(
            cross.at[pl.ds(first, 2), mine, :], from_a.at[k], as_.at[k], ar.at[k], g, to
        )

    cross_arrived(0, 7)
    for p in range(8, 12):
        add_core(p)
    a_copy(0).start()
    a_copy(1).start()
    run_cross(8, 12)
    cross_arrived(7, 12)
    for p in range(4, 8):
        add_core(p)
    a_copy(2).start()
    run_cross(12, 16)

    for p in AROUND[::-1]:
        g1(*p).wait()
    part = pl.ds(c * (TILES // 2) + d * PIECE, PIECE)
    total = gsib[part]
    for dz, dx in AROUND:
        total = total + gred[dz * SIDE + dx]
    gline[pl.ds(y, 1)] = total[None]

    def g2(i):
        return remote(gline.at[y], gline.at[y], g2s.at[i], g2r.at[i], along_y(i, c), d)

    for i in (2, 1, 3):
        g2(i).start()

    cross_arrived(12, 16)
    for p in range(12, 16):
        add_core(p)
    a_copy(3).start()
    for p in range(4):
        add_core(p)

    for i in (1, 3, 2):
        g2(i).wait()
    gtot[part] = (gline[0] + gline[1]) + (gline[2] + gline[3])

    def g3(flip, dz, dx):
        k = flip * SLICES + dz * SIDE + dx
        to_g = other if flip else g
        return remote(gtot.at[part], gtot.at[part], g3s.at[k], g3r.at[k], to_g, chip(dz, dx))

    handed = [(flip, dz, dx) for dz, dx in AROUND for flip in (0, 1)] + [(1, 0, 0)]
    for p in handed:
        g3(*p).start()

    a_copy(0).wait()
    a_copy(1).wait()
    cross[4:6, mine, :] += from_a[0]
    cross[14:16, mine, :] += from_a[1]
    a_copy(4).start()
    a_copy(5).start()
    m[...] = jnp.zeros_like(m)

    for k in range(2, 6):
        a_copy(k).wait()
    cross[0:2, mine, :] += from_a[4] + from_a[3]
    cross[2:4, mine, :] += from_a[2] + from_a[5]

    def b_copy(i):
        return remote(cross.at[i, mine, :], from_b.at[i], bs.at[i], br.at[i], g, along_b(i))

    for i in (2, 1, 3):
        b_copy(i).start()

    for p in handed[::-1]:
        g3(*p).wait()
    for i, j, n, h in PACK:
        block = gtot[8 * n : 8 * n + 8, :, h * BLOCK : (h + 1) * BLOCK].reshape(BLOCK, BLOCK)
        m[i * BLOCK : (i + 1) * BLOCK, j * BLOCK : (j + 1) * BLOCK] = block

    def factor_step(k):
        invert_step(m, k, SK, BLOCK, 16)

    factor_step(0)
    for i in (1, 3, 2):
        b_copy(i).wait()
    line[...] = (cross[0, mine, :] + from_b[1]) + (from_b[2] + from_b[3])

    def y_copy(i):
        rows = pl.ds(pl.multiple_of(lax.rem(y + i, SIDE) * PART, 8), PART)
        return remote(line.at[rows, :], from_y.at[i], ys.at[i], yr.at[i], along_y(i, c), d)

    for i in (2, 1, 3):
        y_copy(i).start()
    factor_step(1)
    factor_step(2)
    for i in (1, 3, 2):
        y_copy(i).wait()
    own = line[pl.ds(pl.multiple_of(y * PART, 8), PART), :]
    final = pl.ds(pl.multiple_of(c * HALF + y * PART, 8), PART)
    cross_out[final, :] = (own + from_y[1]) + (from_y[2] + from_y[3])

    def z_copy(k):
        i, flip = k % SIDE, k // SIDE
        core = c + flip * (1 - 2 * c)
        return remote(
            cross_out.at[final, :], cross_out.at[final, :], zs.at[k], zr.at[k],
            along_y(i, core), d,
        )

    for k in range(1, 2 * SIDE):
        z_copy(k).start()
    factor_step(3)
    factor_step(4)

    high, low = split(m[...] * scale)
    left[...] = jnp.concatenate([high, high, low], axis=1)

    def store(i):
        part = pl.ds(pl.multiple_of(i * STEP, STEP), STEP)
        return pltpu.make_async_copy(out.at[:, part], basis_t.at[:, part], out_sem.at[i])

    def basis_step(i, carry):
        part = pl.ds(pl.multiple_of(i * STEP, STEP), STEP)
        right = jnp.concatenate([parts[:, part], parts[:SK, part]], axis=0)
        out[:, part] = dot(left[...], right, NN)
        store(i).start()
        return carry

    lax.fori_loop(0, LOCAL // STEP, basis_step, 0)
    for k in range(1, 2 * SIDE):
        z_copy(k).wait()
    coeffs[...] = dot3(m[...], cross_out[...], NN) * (1.0 / scale)
    lax.fori_loop(0, LOCAL // STEP, wait_store(store), 0)


def whole_call(scale, slab, map_rows):
    def kernel(*refs):
        whole_kernel(scale, *refs)

    dma = pltpu.SemaphoreType.DMA
    return pl.pallas_call(
        kernel,
        out_shape=(
            jax.ShapeDtypeStruct((SK, LOCAL), F32),
            jax.ShapeDtypeStruct((SK, WIDTH), F32),
        ),
        in_specs=[pl.BlockSpec(memory_space=pltpu.HBM)] * 2,
        out_specs=(
            pl.BlockSpec(memory_space=pl.ANY),
            pl.BlockSpec(memory_space=pltpu.VMEM),
        ),
        scratch_shapes=[
            pltpu.VMEM((SK, SK), F32),
            pltpu.VMEM((SK, WIDTH), F32),
            pltpu.VMEM((SK, 3 * SK), BF16),
            pltpu.VMEM((SK, LOCAL), F32),
            pltpu.VMEM((LOCAL, N), BF16),
            pltpu.VMEM((SK, N), BF16),
            pltpu.VMEM((2 * SK, LOCAL), BF16),
            pltpu.VMEM((TILES, 8, 128), F32),
            pltpu.VMEM((TILES, 8, 128), F32),
            pltpu.VMEM((SLICES, PIECE, 8, 128), F32),
            pltpu.VMEM((SIDE, PIECE, 8, 128), F32),
            pltpu.VMEM((TILES, 8, 128), F32),
            pltpu.VMEM((SLICES, SK, WIDTH), F32),
            pltpu.VMEM((SLICES, HALF, WIDTH), F32),
            pltpu.VMEM((6, 2, HALF, WIDTH), F32),
            pltpu.VMEM((SIDE, HALF, WIDTH), F32),
            pltpu.VMEM((HALF, WIDTH), F32),
            pltpu.VMEM((SIDE, PART, WIDTH), F32),
            dma((LOCAL // CHUNK,)), dma, dma((LOCAL // STEP,)),
            dma, dma,
            dma((SLICES,)), dma((SLICES,)),
            dma((SIDE,)), dma((SIDE,)),
            dma((2 * SLICES,)), dma((2 * SLICES,)),
            dma((SLICES,)), dma((SLICES,)),
            dma((6,)), dma((6,)),
            dma((SIDE,)), dma((SIDE,)),
            dma((SIDE,)), dma((SIDE,)),
            dma((2 * SIDE,)), dma((2 * SIDE,)),
        ],
        compiler_params=pltpu.CompilerParams(
            collective_id=0, has_side_effects=True, vmem_limit_bytes=50 << 20
        ),
        cost_estimate=pl.CostEstimate(
            flops=4 * LOCAL * N * SK, bytes_accessed=24 << 20, transcendentals=0
        ),
        name="range_finder",
    )(slab, map_rows)


def hand_over_kernel(basis_in, coeffs_in, basis_t, coeffs, sem):
    rows = SK // HAND

    def store(i):
        part = pl.ds(i * rows, rows)
        return pltpu.make_async_copy(basis_in.at[part], basis_t.at[part], sem.at[i])

    copies = [store(i) for i in range(HAND)]
    copies.append(pltpu.make_async_copy(coeffs_in, coeffs, sem.at[HAND]))
    for copy in copies:
        copy.start()
    for copy in copies:
        copy.wait()


def hand_over(basis_t, coeffs):
    vmem = pl.BlockSpec(memory_space=pltpu.VMEM)
    hbm = pl.BlockSpec(memory_space=pltpu.HBM)
    return pl.pallas_call(
        hand_over_kernel,
        out_shape=(
            jax.ShapeDtypeStruct((SK, LOCAL), F32),
            jax.ShapeDtypeStruct((SK, WIDTH), F32),
        ),
        in_specs=[vmem, vmem],
        out_specs=(hbm, hbm),
        scratch_shapes=[pltpu.SemaphoreType.DMA((HAND + 1,))],
        compiler_params=pltpu.CompilerParams(vmem_limit_bytes=16 << 20),
        name="hand_over",
    )(basis_t, coeffs)


def local(slab, sketch_map):
    rows = slab.shape[0] * lax.axis_size("grp") * lax.axis_size("dev")
    scale = math.sqrt(rows)
    basis_t, coeffs = hand_over(*whole_call(scale, slab, sketch_map.T))
    return basis_t.T, coeffs


def solution(mesh):
    in_specs = (P(("grp", "dev"), None), P())
    out_specs = (P(("grp", "dev"), None), P(None, "dev"))
    return jax.shard_map(local, mesh=mesh, in_specs=in_specs, out_specs=out_specs, check_vma=False)
```

```python
import math

import jax
import jax.numpy as jnp
from jax import lax
from jax.experimental import pallas as pl
from jax.experimental.pallas import tpu as pltpu
from jax.sharding import PartitionSpec as P

F32 = jnp.float32
BF16 = jnp.bfloat16
NN = (((1,), (0,)), ((), ()))
NT = (((1,), (1,)), ((), ()))
TN = (((0,), (0,)), ((), ()))
MESH = pl.DeviceIdType.MESH

N = 4096
SK = 320
HALF = SK // 2
LOCAL = 2048
CHUNK = 512
STEP = 1024
HAND = 8
WIDTH = 256
SLICES = 16
SIDE = 4


def dot(a, b, dims):
    return lax.dot_general(a, b, dims, preferred_element_type=F32)


def split(a):
    high = a.astype(BF16)
    return high, (a - high.astype(F32)).astype(BF16)


def dot3(a, b, dims):
    ah, al = split(a)
    bh, bl = split(b)
    (ca,), (cb,) = dims[0]
    return dot(jnp.concatenate([ah, al, ah], axis=ca), jnp.concatenate([bh, bh, bl], axis=cb), dims)


def factor_block(a, n, w):
    eye = lax.broadcasted_iota(jnp.int32, (n, n), 0) == lax.broadcasted_iota(jnp.int32, (n, n), 1)
    m = jnp.concatenate([a, eye.astype(F32)], axis=1)
    width = 2 * n
    row_in_group = lax.broadcasted_iota(jnp.int32, (8, width), 0)
    per = w // 8
    groups = [m[8 * g : 8 * g + 8] for g in range(n // 8)]
    done = []

    def spread(value, i):
        return jnp.broadcast_to(value[i : i + 1], (8, width))

    for p in range(n // w):
        rows = groups[p * per :]
        cols = [
            [jnp.broadcast_to(r[:, p * w + l : p * w + l + 1], (8, width)) for r in rows]
            for l in range(w)
        ]
        pivots = [jnp.ones((8, width), F32) for _ in range(per)]
        for k in range(w):
            g, i = divmod(k, 8)
            pivot = spread(cols[k][g], i)
            inverse = 1.0 / pivot
            left = range(g, len(rows))
            factor = {h: cols[k][h] * inverse for h in left}
            factor[g] = jnp.where(row_in_group > i, factor[g], 0.0)
            for l in range(k + 1, w):
                value = spread(cols[l][g], i)
                for h in left:
                    cols[l][h] = cols[l][h] - factor[h] * value
            value = spread(rows[g], i)
            for h in left:
                rows[h] = rows[h] - factor[h] * value
            pivots[g] = jnp.where(row_in_group == i, pivot, pivots[g])
        for h in range(per):
            done.append((rows[h] * lax.rsqrt(pivots[h]))[:, n:])
        groups[p * per :] = rows
    return jnp.concatenate(done, axis=0)


def invert_step(m, k, n, b, w):
    lo, hi = k * b, (k + 1) * b
    t = factor_block(m[lo:hi, lo:hi], b, w)
    r = dot3(t, m[lo:hi, :], NN)
    parts = [r[:, :lo]] if lo else []
    parts.append(t)
    if hi < n:
        parts.append(r[:, hi:])
    r = jnp.concatenate(parts, axis=1)
    if hi < n:
        col = lax.broadcasted_iota(jnp.int32, (n - hi, n), 1)
        keep = jnp.where((col >= lo) & (col < hi), 0.0, m[hi:, :])
        m[hi:, :] = keep - dot3(r[:, hi:], r, TN)
        col = lax.broadcasted_iota(jnp.int32, (b, n), 1)
        r = jnp.where(col < hi, r, 0.0)
    m[lo:hi, :] = r


DIST = (0, 1, 2, 1)
AROUND = sorted(
    ((i, j) for i in range(SIDE) for j in range(SIDE) if (i, j) != (0, 0)),
    key=lambda p: -(DIST[p[0]] + DIST[p[1]]),
)
CELLS = (
    [(2, j) for j in range(4)] + [(0, 2), (1, 2), (3, 2)]
    + [(1, 0), (1, 1), (1, 3), (0, 1), (3, 1)]
    + [(3, 0), (3, 3), (0, 3)]
    + [(0, 0)]
)
BLOCK = 64
EVEN = [(i, j) for j in (0, 2, 4) for i in range(j + 1)]
ODD = [(i, j) for j in (1, 3) for i in range(j + 1)]
PACK = [(i, j, n, 0) for n, (i, j) in enumerate(EVEN[:8])]
PACK += [(i, j, n, 1) for n, (i, j) in enumerate(ODD + EVEN[8:])]
TILES = 64
PIECE = TILES // 32
PART = HALF // SIDE


def wait_store(store):
    def body(i, carry):
        store(i).wait()
        return carry

    return body


def table(q, values):
    return sum(jnp.where(q == k, v, 0) for k, v in enumerate(values) if v)


def whole_kernel(
    scale, slab, map_rows,
    basis_t, coeffs,
    m, cross_out, left, out, slab_v, map_t, parts, gpack, gsib, gred, gline, gtot,
    cross, from_core, from_a, from_b, line, from_y,
    load_sem, map_sem, out_sem,
    g0s, g0r, g1s, g1r, g2s, g2r, g3s, g3r,
    xs, xr, as_, ar, bs, br, ys, yr, zs, zr,
):
    g = lax.axis_index("grp")
    d = lax.axis_index("dev")
    y, c = g // 2, g % 2
    z, x = d // SIDE, d % SIDE
    other = g + 1 - 2 * c
    row_c = pl.multiple_of(c * HALF, 8)
    row_o = pl.multiple_of((1 - c) * HALF, 8)
    mine = pl.ds(row_c, HALF)

    map_copy = pltpu.make_async_copy(map_rows, map_t, map_sem)
    map_copy.start()

    def load(i):
        rows = pl.ds(pl.multiple_of(i * CHUNK, CHUNK), CHUNK)
        return pltpu.make_async_copy(slab.at[rows, :], slab_v.at[rows, :], load_sem.at[i])

    load(0).start()
    load(1).start()

    def chip(dz, dx):
        return lax.rem(z + dz, SIDE) * SIDE + lax.rem(x + dx, SIDE)

    def along_a(i):
        return jnp.where(c == 0, chip(i, 0), chip(0, i))

    def along_b(i):
        return jnp.where(c == 0, chip(0, i), chip(i, 0))

    def along_y(i, core):
        return lax.rem(y + i, SIDE) * 2 + core

    barrier = pltpu.get_barrier_semaphore()

    def greet(to_g, to_d):
        pl.semaphore_signal(barrier, inc=1, device_id=(to_g, to_d), device_id_type=MESH)

    for dz, dx in AROUND:
        greet(g, chip(dz, dx))
        greet(other, chip(dz, dx))
    for i in range(1, SIDE):
        greet(along_y(i, c), d)
    for i in range(SIDE):
        greet(along_y(i, 1 - c), d)

    map_copy.wait()

    def sketch_chunk(i, carry):
        load(i).wait()

        @pl.when(i + 2 < LOCAL // CHUNK)
        def _():
            load(i + 2).start()

        rows = pl.ds(pl.multiple_of(i * CHUNK, CHUNK), CHUNK)
        s = dot(map_t[...], slab_v[rows, :], NT)
        high, low = split(s)
        parts[:SK, rows] = high
        parts[SK:, rows] = low
        return carry

    lax.fori_loop(0, LOCAL // CHUNK, sketch_chunk, 0)

    mixed = dot(parts[SK:], parts[:SK], NT)
    gram = dot(parts[:SK], parts[:SK], NT) + (mixed + mixed.T)
    gpack[56:64] = jnp.zeros((8, 8, 128), F32)
    for i, j, n, h in PACK:
        block = gram[i * BLOCK : (i + 1) * BLOCK, j * BLOCK : (j + 1) * BLOCK]
        gpack[8 * n : 8 * n + 8, :, h * BLOCK : (h + 1) * BLOCK] = block.reshape(8, 8, BLOCK)

    pl.semaphore_wait(barrier, 2 * len(AROUND) + 2 * SIDE - 1)

    def remote(src, dst, send, recv, to_g, to_d):
        return pltpu.make_async_remote_copy(
            src_ref=src, dst_ref=dst, send_sem=send, recv_sem=recv,
            device_id=(to_g, to_d), device_id_type=MESH,
        )

    def core_copy(q):
        dz, dx = table(q, [p[0] for p in CELLS]), table(q, [p[1] for p in CELLS])
        here = jnp.where(c == 0, dz * SIDE + dx, dx * SIDE + dz)
        there = jnp.where(c == 0, dx * SIDE + dz, dz * SIDE + dx)
        return remote(
            cross.at[here, pl.ds(row_o, HALF), :], from_core.at[there],
            xs.at[q], xr.at[q], other, d,
        )

    def cross_cell(q):
        dz, dx = table(q, [p[0] for p in CELLS]), table(q, [p[1] for p in CELLS])
        here = jnp.where(c == 0, dz * SIDE + dx, dx * SIDE + dz)
        columns = pl.ds(pl.multiple_of(chip(dz, dx) * WIDTH, WIDTH), WIDTH)
        return here, dot(parts[:SK], slab_v[:, columns], NN)

    def cross_pair(t, carry):
        first, a = cross_cell(2 * t)
        second, b = cross_cell(2 * t + 1)
        cross[first] = a
        cross[second] = b
        core_copy(2 * t).start()
        core_copy(2 * t + 1).start()
        return carry

    def run_cross(first, last):
        lax.fori_loop(first // 2, last // 2, cross_pair, 0)

    def cross_arrived(first, last):
        def body(q, carry):
            core_copy(q).wait()
            return carry
        lax.fori_loop(first, last, body, 0)

    def add_core(p):
        cross[p, mine, :] += from_core[p]

    g0 = remote(gpack, gsib, g0s, g0r, other, d)
    g0.start()
    run_cross(0, 4)
    g0.wait()
    gsib[...] = gpack[...] + gsib[...]

    def g1(dz, dx):
        to = chip(dz, dx)
        k = dz * SIDE + dx
        part = pl.ds(c * (TILES // 2) + to * PIECE, PIECE)
        return remote(gsib.at[part], gred.at[k], g1s.at[k], g1r.at[k], g, to)

    for p in AROUND:
        g1(*p).start()
    run_cross(4, 8)

    def a_copy(k):
        first = (8, 10, 6, 12, 4, 14)[k]
        to = along_a(1 if k % 2 == 0 else SIDE - 1)
        return remote(
            cross.at[pl.ds(first, 2), mine, :], from_a.at[k], as_.at[k], ar.at[k], g, to
        )

    cross_arrived(0, 7)
    for p in range(8, 12):
        add_core(p)
    a_copy(0).start()
    a_copy(1).start()
    run_cross(8, 12)
    cross_arrived(7, 12)
    for p in range(4, 8):
        add_core(p)
    a_copy(2).start()
    run_cross(12, 16)

    for p in AROUND[::-1]:
        g1(*p).wait()
    part = pl.ds(c * (TILES // 2) + d * PIECE, PIECE)
    total = gsib[part]
    for dz, dx in AROUND:
        total = total + gred[dz * SIDE + dx]
    gline[pl.ds(y, 1)] = total[None]

    def g2(i):
        return remote(gline.at[y], gline.at[y], g2s.at[i], g2r.at[i], along_y(i, c), d)

    for i in (2, 1, 3):
        g2(i).start()

    cross_arrived(12, 16)
    for p in range(12, 16):
        add_core(p)
    a_copy(3).start()
    a_copy(0).wait()
    a_copy(1).wait()
    cross[4:6, mine, :] += from_a[0]
    cross[14:16, mine, :] += from_a[1]
    a_copy(4).start()
    a_copy(5).start()
    for p in range(4):
        add_core(p)

    for i in (1, 3, 2):
        g2(i).wait()
    gtot[part] = (gline[0] + gline[1]) + (gline[2] + gline[3])

    def g3(flip, dz, dx):
        k = flip * SLICES + dz * SIDE + dx
        to_g = other if flip else g
        return remote(gtot.at[part], gtot.at[part], g3s.at[k], g3r.at[k], to_g, chip(dz, dx))

    handed = [(flip, dz, dx) for dz, dx in AROUND for flip in (0, 1)] + [(1, 0, 0)]
    for p in handed:
        g3(*p).start()

    m[...] = jnp.zeros_like(m)

    for k in range(2, 6):
        a_copy(k).wait()
    cross[0:2, mine, :] += from_a[4] + from_a[3]
    cross[2:4, mine, :] += from_a[2] + from_a[5]

    def b_copy(i):
        return remote(cross.at[i, mine, :], from_b.at[i], bs.at[i], br.at[i], g, along_b(i))

    for i in (2, 1, 3):
        b_copy(i).start()

    for p in handed[::-1]:
        g3(*p).wait()
    for i, j, n, h in PACK:
        block = gtot[8 * n : 8 * n + 8, :, h * BLOCK : (h + 1) * BLOCK].reshape(BLOCK, BLOCK)
        m[i * BLOCK : (i + 1) * BLOCK, j * BLOCK : (j + 1) * BLOCK] = block

    def factor_step(k):
        invert_step(m, k, SK, BLOCK, 16)

    factor_step(0)
    for i in (1, 3, 2):
        b_copy(i).wait()
    line[...] = (cross[0, mine, :] + from_b[1]) + (from_b[2] + from_b[3])

    def y_copy(i):
        rows = pl.ds(pl.multiple_of(lax.rem(y + i, SIDE) * PART, 8), PART)
        return remote(line.at[rows, :], from_y.at[i], ys.at[i], yr.at[i], along_y(i, c), d)

    for i in (2, 1, 3):
        y_copy(i).start()
    factor_step(1)
    factor_step(2)
    for i in (1, 3, 2):
        y_copy(i).wait()
    own = line[pl.ds(pl.multiple_of(y * PART, 8), PART), :]
    final = pl.ds(pl.multiple_of(c * HALF + y * PART, 8), PART)
    cross_out[final, :] = (own + from_y[1]) + (from_y[2] + from_y[3])

    def z_copy(k):
        i, flip = k % SIDE, k // SIDE
        core = c + flip * (1 - 2 * c)
        return remote(
            cross_out.at[final, :], cross_out.at[final, :], zs.at[k], zr.at[k],
            along_y(i, core), d,
        )

    for k in range(1, 2 * SIDE):
        z_copy(k).start()
    factor_step(3)
    factor_step(4)

    high, low = split(m[...] * scale)
    left[...] = jnp.concatenate([high, high, low], axis=1)

    def store(i):
        part = pl.ds(pl.multiple_of(i * STEP, STEP), STEP)
        return pltpu.make_async_copy(out.at[:, part], basis_t.at[:, part], out_sem.at[i])

    def basis_step(i, carry):
        part = pl.ds(pl.multiple_of(i * STEP, STEP), STEP)
        right = jnp.concatenate([parts[:, part], parts[:SK, part]], axis=0)
        out[:, part] = dot(left[...], right, NN)
        store(i).start()
        return carry

    lax.fori_loop(0, LOCAL // STEP, basis_step, 0)
    for k in range(1, 2 * SIDE):
        z_copy(k).wait()
    coeffs[...] = dot3(m[...], cross_out[...], NN) * (1.0 / scale)
    lax.fori_loop(0, LOCAL // STEP, wait_store(store), 0)


def whole_call(scale, slab, map_rows):
    def kernel(*refs):
        whole_kernel(scale, *refs)

    dma = pltpu.SemaphoreType.DMA
    return pl.pallas_call(
        kernel,
        out_shape=(
            jax.ShapeDtypeStruct((SK, LOCAL), F32),
            jax.ShapeDtypeStruct((SK, WIDTH), F32),
        ),
        in_specs=[pl.BlockSpec(memory_space=pltpu.HBM)] * 2,
        out_specs=(
            pl.BlockSpec(memory_space=pl.ANY),
            pl.BlockSpec(memory_space=pltpu.VMEM),
        ),
        scratch_shapes=[
            pltpu.VMEM((SK, SK), F32),
            pltpu.VMEM((SK, WIDTH), F32),
            pltpu.VMEM((SK, 3 * SK), BF16),
            pltpu.VMEM((SK, LOCAL), F32),
            pltpu.VMEM((LOCAL, N), BF16),
            pltpu.VMEM((SK, N), BF16),
            pltpu.VMEM((2 * SK, LOCAL), BF16),
            pltpu.VMEM((TILES, 8, 128), F32),
            pltpu.VMEM((TILES, 8, 128), F32),
            pltpu.VMEM((SLICES, PIECE, 8, 128), F32),
            pltpu.VMEM((SIDE, PIECE, 8, 128), F32),
            pltpu.VMEM((TILES, 8, 128), F32),
            pltpu.VMEM((SLICES, SK, WIDTH), F32),
            pltpu.VMEM((SLICES, HALF, WIDTH), F32),
            pltpu.VMEM((6, 2, HALF, WIDTH), F32),
            pltpu.VMEM((SIDE, HALF, WIDTH), F32),
            pltpu.VMEM((HALF, WIDTH), F32),
            pltpu.VMEM((SIDE, PART, WIDTH), F32),
            dma((LOCAL // CHUNK,)), dma, dma((LOCAL // STEP,)),
            dma, dma,
            dma((SLICES,)), dma((SLICES,)),
            dma((SIDE,)), dma((SIDE,)),
            dma((2 * SLICES,)), dma((2 * SLICES,)),
            dma((SLICES,)), dma((SLICES,)),
            dma((6,)), dma((6,)),
            dma((SIDE,)), dma((SIDE,)),
            dma((SIDE,)), dma((SIDE,)),
            dma((2 * SIDE,)), dma((2 * SIDE,)),
        ],
        compiler_params=pltpu.CompilerParams(
            collective_id=0, has_side_effects=True, vmem_limit_bytes=50 << 20
        ),
        cost_estimate=pl.CostEstimate(
            flops=4 * LOCAL * N * SK, bytes_accessed=24 << 20, transcendentals=0
        ),
        name="range_finder",
    )(slab, map_rows)


def hand_over_kernel(basis_in, coeffs_in, basis_t, coeffs, sem):
    rows = SK // HAND

    def store(i):
        part = pl.ds(i * rows, rows)
        return pltpu.make_async_copy(basis_in.at[part], basis_t.at[part], sem.at[i])

    copies = [store(i) for i in range(HAND)]
    copies.append(pltpu.make_async_copy(coeffs_in, coeffs, sem.at[HAND]))
    for copy in copies:
        copy.start()
    for copy in copies:
        copy.wait()


def hand_over(basis_t, coeffs):
    vmem = pl.BlockSpec(memory_space=pltpu.VMEM)
    hbm = pl.BlockSpec(memory_space=pltpu.HBM)
    return pl.pallas_call(
        hand_over_kernel,
        out_shape=(
            jax.ShapeDtypeStruct((SK, LOCAL), F32),
            jax.ShapeDtypeStruct((SK, WIDTH), F32),
        ),
        in_specs=[vmem, vmem],
        out_specs=(hbm, hbm),
        scratch_shapes=[pltpu.SemaphoreType.DMA((HAND + 1,))],
        compiler_params=pltpu.CompilerParams(vmem_limit_bytes=16 << 20),
        name="hand_over",
    )(basis_t, coeffs)


def local(slab, sketch_map):
    rows = slab.shape[0] * lax.axis_size("grp") * lax.axis_size("dev")
    scale = math.sqrt(rows)
    basis_t, coeffs = hand_over(*whole_call(scale, slab, sketch_map.T))
    return basis_t.T, coeffs


def solution(mesh):
    in_specs = (P(("grp", "dev"), None), P())
    out_specs = (P(("grp", "dev"), None), P(None, "dev"))
    return jax.shard_map(local, mesh=mesh, in_specs=in_specs, out_specs=out_specs, check_vma=False)
```

```python
import math

import jax
import jax.numpy as jnp
from jax import lax
from jax.experimental import pallas as pl
from jax.experimental.pallas import tpu as pltpu
from jax.sharding import PartitionSpec as P

F32 = jnp.float32
BF16 = jnp.bfloat16
NN = (((1,), (0,)), ((), ()))
NT = (((1,), (1,)), ((), ()))
TN = (((0,), (0,)), ((), ()))
MESH = pl.DeviceIdType.MESH

N = 4096
SK = 320
HALF = SK // 2
LOCAL = 2048
CHUNK = 512
STEP = 1024
HAND = 8
WIDTH = 256
SLICES = 16
SIDE = 4


def dot(a, b, dims):
    return lax.dot_general(a, b, dims, preferred_element_type=F32)


def split(a):
    high = a.astype(BF16)
    return high, (a - high.astype(F32)).astype(BF16)


def dot3(a, b, dims):
    ah, al = split(a)
    bh, bl = split(b)
    (ca,), (cb,) = dims[0]
    return dot(jnp.concatenate([ah, al, ah], axis=ca), jnp.concatenate([bh, bh, bl], axis=cb), dims)


def factor_block(a, n, w):
    eye = lax.broadcasted_iota(jnp.int32, (n, n), 0) == lax.broadcasted_iota(jnp.int32, (n, n), 1)
    m = jnp.concatenate([a, eye.astype(F32)], axis=1)
    width = 2 * n
    row_in_group = lax.broadcasted_iota(jnp.int32, (8, width), 0)
    per = w // 8
    groups = [m[8 * g : 8 * g + 8] for g in range(n // 8)]
    done = []

    def spread(value, i):
        return jnp.broadcast_to(value[i : i + 1], (8, width))

    for p in range(n // w):
        rows = groups[p * per :]
        cols = [
            [jnp.broadcast_to(r[:, p * w + l : p * w + l + 1], (8, width)) for r in rows]
            for l in range(w)
        ]
        pivots = [jnp.ones((8, width), F32) for _ in range(per)]
        for k in range(w):
            g, i = divmod(k, 8)
            pivot = spread(cols[k][g], i)
            inverse = 1.0 / pivot
            left = range(g, len(rows))
            factor = {h: cols[k][h] * inverse for h in left}
            factor[g] = jnp.where(row_in_group > i, factor[g], 0.0)
            for l in range(k + 1, w):
                value = spread(cols[l][g], i)
                for h in left:
                    cols[l][h] = cols[l][h] - factor[h] * value
            value = spread(rows[g], i)
            for h in left:
                rows[h] = rows[h] - factor[h] * value
            pivots[g] = jnp.where(row_in_group == i, pivot, pivots[g])
        for h in range(per):
            done.append((rows[h] * lax.rsqrt(pivots[h]))[:, n:])
        groups[p * per :] = rows
    return jnp.concatenate(done, axis=0)


def invert_step(m, k, n, b, w):
    lo, hi = k * b, (k + 1) * b
    t = factor_block(m[lo:hi, lo:hi], b, w)
    r = dot3(t, m[lo:hi, :], NN)
    parts = [r[:, :lo]] if lo else []
    parts.append(t)
    if hi < n:
        parts.append(r[:, hi:])
    r = jnp.concatenate(parts, axis=1)
    if hi < n:
        col = lax.broadcasted_iota(jnp.int32, (n - hi, n), 1)
        keep = jnp.where((col >= lo) & (col < hi), 0.0, m[hi:, :])
        m[hi:, :] = keep - dot3(r[:, hi:], r, TN)
        col = lax.broadcasted_iota(jnp.int32, (b, n), 1)
        r = jnp.where(col < hi, r, 0.0)
    m[lo:hi, :] = r


DIST = (0, 1, 2, 1)
AROUND = sorted(
    ((i, j) for i in range(SIDE) for j in range(SIDE) if (i, j) != (0, 0)),
    key=lambda p: -(DIST[p[0]] + DIST[p[1]]),
)
CELLS = (
    [(2, j) for j in range(4)] + [(0, 2), (1, 2), (3, 2)]
    + [(1, 0), (1, 1), (1, 3), (0, 1), (3, 1)]
    + [(3, 0), (3, 3), (0, 3)]
    + [(0, 0)]
)
BLOCK = 64
EVEN = [(i, j) for j in (0, 2, 4) for i in range(j + 1)]
ODD = [(i, j) for j in (1, 3) for i in range(j + 1)]
PACK = [(i, j, n, 0) for n, (i, j) in enumerate(EVEN[:8])]
PACK += [(i, j, n, 1) for n, (i, j) in enumerate(ODD + EVEN[8:])]
TILES = 64
PIECE = TILES // 32
PART = HALF // SIDE


def wait_store(store):
    def body(i, carry):
        store(i).wait()
        return carry

    return body


def table(q, values):
    return sum(jnp.where(q == k, v, 0) for k, v in enumerate(values) if v)


def whole_kernel(
    scale, slab, map_rows,
    basis_t, coeffs,
    m, cross_out, left, out, slab_v, map_t, parts, gpack, gsib, gred, gline, gtot,
    cross, from_core, from_a, from_b, line, from_y,
    load_sem, map_sem, out_sem,
    g0s, g0r, g1s, g1r, g2s, g2r, g3s, g3r,
    xs, xr, as_, ar, bs, br, ys, yr, zs, zr,
):
    g = lax.axis_index("grp")
    d = lax.axis_index("dev")
    y, c = g // 2, g % 2
    z, x = d // SIDE, d % SIDE
    other = g + 1 - 2 * c
    row_c = pl.multiple_of(c * HALF, 8)
    row_o = pl.multiple_of((1 - c) * HALF, 8)
    mine = pl.ds(row_c, HALF)

    map_copy = pltpu.make_async_copy(map_rows, map_t, map_sem)
    map_copy.start()

    def load(i):
        rows = pl.ds(pl.multiple_of(i * CHUNK, CHUNK), CHUNK)
        return pltpu.make_async_copy(slab.at[rows, :], slab_v.at[rows, :], load_sem.at[i])

    load(0).start()
    load(1).start()

    def chip(dz, dx):
        return lax.rem(z + dz, SIDE) * SIDE + lax.rem(x + dx, SIDE)

    def along_a(i):
        return jnp.where(c == 0, chip(i, 0), chip(0, i))

    def along_b(i):
        return jnp.where(c == 0, chip(0, i), chip(i, 0))

    def along_y(i, core):
        return lax.rem(y + i, SIDE) * 2 + core

    barrier = pltpu.get_barrier_semaphore()

    def greet(to_g, to_d):
        pl.semaphore_signal(barrier, inc=1, device_id=(to_g, to_d), device_id_type=MESH)

    for dz, dx in AROUND:
        greet(g, chip(dz, dx))
        greet(other, chip(dz, dx))
    for i in range(1, SIDE):
        greet(along_y(i, c), d)
    for i in range(SIDE):
        greet(along_y(i, 1 - c), d)

    map_copy.wait()

    def sketch_chunk(i, carry):
        load(i).wait()

        @pl.when(i + 2 < LOCAL // CHUNK)
        def _():
            load(i + 2).start()

        rows = pl.ds(pl.multiple_of(i * CHUNK, CHUNK), CHUNK)
        s = dot(map_t[...], slab_v[rows, :], NT)
        high, low = split(s)
        parts[:SK, rows] = high
        parts[SK:, rows] = low
        return carry

    lax.fori_loop(0, LOCAL // CHUNK, sketch_chunk, 0)

    mixed = dot(parts[SK:], parts[:SK], NT)
    gram = dot(parts[:SK], parts[:SK], NT) + (mixed + mixed.T)
    gpack[56:64] = jnp.zeros((8, 8, 128), F32)
    for i, j, n, h in PACK:
        block = gram[i * BLOCK : (i + 1) * BLOCK, j * BLOCK : (j + 1) * BLOCK]
        gpack[8 * n : 8 * n + 8, :, h * BLOCK : (h + 1) * BLOCK] = block.reshape(8, 8, BLOCK)

    pl.semaphore_wait(barrier, 2 * len(AROUND) + 2 * SIDE - 1)

    def remote(src, dst, send, recv, to_g, to_d):
        return pltpu.make_async_remote_copy(
            src_ref=src, dst_ref=dst, send_sem=send, recv_sem=recv,
            device_id=(to_g, to_d), device_id_type=MESH,
        )

    def core_copy(q):
        dz, dx = table(q, [p[0] for p in CELLS]), table(q, [p[1] for p in CELLS])
        here = jnp.where(c == 0, dz * SIDE + dx, dx * SIDE + dz)
        there = jnp.where(c == 0, dx * SIDE + dz, dz * SIDE + dx)
        return remote(
            cross.at[here, pl.ds(row_o, HALF), :], from_core.at[there],
            xs.at[q], xr.at[q], other, d,
        )

    def cross_cell(q):
        dz, dx = table(q, [p[0] for p in CELLS]), table(q, [p[1] for p in CELLS])
        here = jnp.where(c == 0, dz * SIDE + dx, dx * SIDE + dz)
        columns = pl.ds(pl.multiple_of(chip(dz, dx) * WIDTH, WIDTH), WIDTH)
        return here, dot(parts[:SK], slab_v[:, columns], NN)

    def cross_pair(t, carry):
        first, a = cross_cell(2 * t)
        second, b = cross_cell(2 * t + 1)
        cross[first] = a
        cross[second] = b
        core_copy(2 * t).start()
        core_copy(2 * t + 1).start()
        return carry

    def run_cross(first, last):
        lax.fori_loop(first // 2, last // 2, cross_pair, 0)

    def cross_arrived(first, last):
        def body(q, carry):
            core_copy(q).wait()
            return carry
        lax.fori_loop(first, last, body, 0)

    def add_core(p):
        cross[p, mine, :] += from_core[p]

    g0 = remote(gpack, gsib, g0s, g0r, other, d)
    g0.start()
    run_cross(0, 4)
    g0.wait()
    gsib[...] = gpack[...] + gsib[...]

    def g1(dz, dx):
        to = chip(dz, dx)
        k = dz * SIDE + dx
        part = pl.ds(c * (TILES // 2) + to * PIECE, PIECE)
        return remote(gsib.at[part], gred.at[k], g1s.at[k], g1r.at[k], g, to)

    for p in AROUND:
        g1(*p).start()
    run_cross(4, 8)

    def a_copy(k):
        first = (8, 10, 6, 12, 4, 14)[k]
        to = along_a(1 if k % 2 == 0 else SIDE - 1)
        return remote(
            cross.at[pl.ds(first, 2), mine, :], from_a.at[k], as_.at[k], ar.at[k], g, to
        )

    cross_arrived(0, 7)
    for p in range(8, 12):
        add_core(p)
    a_copy(0).start()
    a_copy(1).start()
    run_cross(8, 12)
    cross_arrived(7, 12)
    for p in range(4, 8):
        add_core(p)
    a_copy(2).start()
    run_cross(12, 16)
    cross_arrived(12, 16)
    for p in range(12, 16):
        add_core(p)
    a_copy(3).start()

    for p in AROUND[::-1]:
        g1(*p).wait()
    part = pl.ds(c * (TILES // 2) + d * PIECE, PIECE)
    total = gsib[part]
    for dz, dx in AROUND:
        total = total + gred[dz * SIDE + dx]
    gline[pl.ds(y, 1)] = total[None]

    def g2(i):
        return remote(gline.at[y], gline.at[y], g2s.at[i], g2r.at[i], along_y(i, c), d)

    for i in (2, 1, 3):
        g2(i).start()

    a_copy(0).wait()
    a_copy(1).wait()
    cross[4:6, mine, :] += from_a[0]
    cross[14:16, mine, :] += from_a[1]
    a_copy(4).start()
    a_copy(5).start()
    for p in range(4):
        add_core(p)

    for i in (1, 3, 2):
        g2(i).wait()
    gtot[part] = (gline[0] + gline[1]) + (gline[2] + gline[3])

    def g3(flip, dz, dx):
        k = flip * SLICES + dz * SIDE + dx
        to_g = other if flip else g
        return remote(gtot.at[part], gtot.at[part], g3s.at[k], g3r.at[k], to_g, chip(dz, dx))

    handed = [(flip, dz, dx) for dz, dx in AROUND for flip in (0, 1)] + [(1, 0, 0)]
    for p in handed:
        g3(*p).start()

    m[...] = jnp.zeros_like(m)

    for k in range(2, 6):
        a_copy(k).wait()
    cross[0:2, mine, :] += from_a[4] + from_a[3]
    cross[2:4, mine, :] += from_a[2] + from_a[5]

    def b_copy(i):
        return remote(cross.at[i, mine, :], from_b.at[i], bs.at[i], br.at[i], g, along_b(i))

    for i in (2, 1, 3):
        b_copy(i).start()

    for p in handed[::-1]:
        g3(*p).wait()
    for i, j, n, h in PACK:
        block = gtot[8 * n : 8 * n + 8, :, h * BLOCK : (h + 1) * BLOCK].reshape(BLOCK, BLOCK)
        m[i * BLOCK : (i + 1) * BLOCK, j * BLOCK : (j + 1) * BLOCK] = block

    def factor_step(k):
        invert_step(m, k, SK, BLOCK, 16)

    factor_step(0)
    for i in (1, 3, 2):
        b_copy(i).wait()
    line[...] = (cross[0, mine, :] + from_b[1]) + (from_b[2] + from_b[3])

    def y_copy(i):
        rows = pl.ds(pl.multiple_of(lax.rem(y + i, SIDE) * PART, 8), PART)
        return remote(line.at[rows, :], from_y.at[i], ys.at[i], yr.at[i], along_y(i, c), d)

    for i in (2, 1, 3):
        y_copy(i).start()
    factor_step(1)
    factor_step(2)
    for i in (1, 3, 2):
        y_copy(i).wait()
    own = line[pl.ds(pl.multiple_of(y * PART, 8), PART), :]
    final = pl.ds(pl.multiple_of(c * HALF + y * PART, 8), PART)
    cross_out[final, :] = (own + from_y[1]) + (from_y[2] + from_y[3])

    def z_copy(k):
        i, flip = k % SIDE, k // SIDE
        core = c + flip * (1 - 2 * c)
        return remote(
            cross_out.at[final, :], cross_out.at[final, :], zs.at[k], zr.at[k],
            along_y(i, core), d,
        )

    for k in range(1, 2 * SIDE):
        z_copy(k).start()
    factor_step(3)
    factor_step(4)

    high, low = split(m[...] * scale)
    left[...] = jnp.concatenate([high, high, low], axis=1)

    def store(i):
        part = pl.ds(pl.multiple_of(i * STEP, STEP), STEP)
        return pltpu.make_async_copy(out.at[:, part], basis_t.at[:, part], out_sem.at[i])

    def basis_step(i, carry):
        part = pl.ds(pl.multiple_of(i * STEP, STEP), STEP)
        right = jnp.concatenate([parts[:, part], parts[:SK, part]], axis=0)
        out[:, part] = dot(left[...], right, NN)
        store(i).start()
        return carry

    lax.fori_loop(0, LOCAL // STEP, basis_step, 0)
    for k in range(1, 2 * SIDE):
        z_copy(k).wait()
    coeffs[...] = dot3(m[...], cross_out[...], NN) * (1.0 / scale)
    lax.fori_loop(0, LOCAL // STEP, wait_store(store), 0)


def whole_call(scale, slab, map_rows):
    def kernel(*refs):
        whole_kernel(scale, *refs)

    dma = pltpu.SemaphoreType.DMA
    return pl.pallas_call(
        kernel,
        out_shape=(
            jax.ShapeDtypeStruct((SK, LOCAL), F32),
            jax.ShapeDtypeStruct((SK, WIDTH), F32),
        ),
        in_specs=[pl.BlockSpec(memory_space=pltpu.HBM)] * 2,
        out_specs=(
            pl.BlockSpec(memory_space=pl.ANY),
            pl.BlockSpec(memory_space=pltpu.VMEM),
        ),
        scratch_shapes=[
            pltpu.VMEM((SK, SK), F32),
            pltpu.VMEM((SK, WIDTH), F32),
            pltpu.VMEM((SK, 3 * SK), BF16),
            pltpu.VMEM((SK, LOCAL), F32),
            pltpu.VMEM((LOCAL, N), BF16),
            pltpu.VMEM((SK, N), BF16),
            pltpu.VMEM((2 * SK, LOCAL), BF16),
            pltpu.VMEM((TILES, 8, 128), F32),
            pltpu.VMEM((TILES, 8, 128), F32),
            pltpu.VMEM((SLICES, PIECE, 8, 128), F32),
            pltpu.VMEM((SIDE, PIECE, 8, 128), F32),
            pltpu.VMEM((TILES, 8, 128), F32),
            pltpu.VMEM((SLICES, SK, WIDTH), F32),
            pltpu.VMEM((SLICES, HALF, WIDTH), F32),
            pltpu.VMEM((6, 2, HALF, WIDTH), F32),
            pltpu.VMEM((SIDE, HALF, WIDTH), F32),
            pltpu.VMEM((HALF, WIDTH), F32),
            pltpu.VMEM((SIDE, PART, WIDTH), F32),
            dma((LOCAL // CHUNK,)), dma, dma((LOCAL // STEP,)),
            dma, dma,
            dma((SLICES,)), dma((SLICES,)),
            dma((SIDE,)), dma((SIDE,)),
            dma((2 * SLICES,)), dma((2 * SLICES,)),
            dma((SLICES,)), dma((SLICES,)),
            dma((6,)), dma((6,)),
            dma((SIDE,)), dma((SIDE,)),
            dma((SIDE,)), dma((SIDE,)),
            dma((2 * SIDE,)), dma((2 * SIDE,)),
        ],
        compiler_params=pltpu.CompilerParams(
            collective_id=0, has_side_effects=True, vmem_limit_bytes=50 << 20
        ),
        cost_estimate=pl.CostEstimate(
            flops=4 * LOCAL * N * SK, bytes_accessed=24 << 20, transcendentals=0
        ),
        name="range_finder",
    )(slab, map_rows)


def hand_over_kernel(basis_in, coeffs_in, basis_t, coeffs, sem):
    rows = SK // HAND

    def store(i):
        part = pl.ds(i * rows, rows)
        return pltpu.make_async_copy(basis_in.at[part], basis_t.at[part], sem.at[i])

    copies = [store(i) for i in range(HAND)]
    copies.append(pltpu.make_async_copy(coeffs_in, coeffs, sem.at[HAND]))
    for copy in copies:
        copy.start()
    for copy in copies:
        copy.wait()


def hand_over(basis_t, coeffs):
    vmem = pl.BlockSpec(memory_space=pltpu.VMEM)
    hbm = pl.BlockSpec(memory_space=pltpu.HBM)
    return pl.pallas_call(
        hand_over_kernel,
        out_shape=(
            jax.ShapeDtypeStruct((SK, LOCAL), F32),
            jax.ShapeDtypeStruct((SK, WIDTH), F32),
        ),
        in_specs=[vmem, vmem],
        out_specs=(hbm, hbm),
        scratch_shapes=[pltpu.SemaphoreType.DMA((HAND + 1,))],
        compiler_params=pltpu.CompilerParams(vmem_limit_bytes=16 << 20),
        name="hand_over",
    )(basis_t, coeffs)


def local(slab, sketch_map):
    rows = slab.shape[0] * lax.axis_size("grp") * lax.axis_size("dev")
    scale = math.sqrt(rows)
    basis_t, coeffs = hand_over(*whole_call(scale, slab, sketch_map.T))
    return basis_t.T, coeffs


def solution(mesh):
    in_specs = (P(("grp", "dev"), None), P())
    out_specs = (P(("grp", "dev"), None), P(None, "dev"))
    return jax.shard_map(local, mesh=mesh, in_specs=in_specs, out_specs=out_specs, check_vma=False)
```
